128 devices in a mesh: lat: 8 (over x, y_hi), lon: 16 (over z, y_lo, core).
Axes of the slice: x: 4, y: 4 (y_hi: 2, y_lo: 2; y = y_hi * 2 + y_lo), z: 4, core: 2. Of those that a mesh axis runs over, the one named last changes fastest.
Arguments:
- latent_field: bfloat16 [192, 2, 96, 512], P('lon', None, 'lat'), may hold values from -6 to 6
- sensitivity: bfloat16 [192, 2, 96, 512], P('lon', None, 'lat'), may hold values from -6 to 6
- first_gain: float32 [512], replicated, may hold values from 0.1 to 1.9
- first_proj: bfloat16 [4, 512, 512], replicated, may hold values from -8 to 8
- merge_gain: float32 [2048], replicated, may hold values from 0.1 to 1.9
- merge_weight: bfloat16 [2048, 1024], replicated, may hold values from -0.125 to 0.125
- middle_gain: float32 [1024], replicated, may hold values from 0.1 to 1.9
- middle_proj: bfloat16 [4, 1024, 1024], P(None, None, 'lon'), may hold values from -8 to 8
- reduce_gain: float32 [4096], replicated, may hold values from 0.1 to 1.9
- reduce_weight: bfloat16 [4096, 2048], P(None, 'lon'), may hold values from -0.09375 to 0.09375
- coarse_gain: float32 [2048], replicated, may hold values from 0.1 to 1.9
- coarse_proj: bfloat16 [4, 2048, 2048], P(None, None, 'lon'), may hold values from -8 to 8
- lift_gain: float32 [2048], replicated, may hold values from 0.1 to 1.9
- lift_weight: bfloat16 [2048, 4096], P(None, 'lon'), may hold values from -0.125 to 0.125
- widen_gain: float32 [1024], replicated, may hold values from 0.1 to 1.9
- widen_weight: bfloat16 [1024, 2048], replicated, may hold values from -0.1875 to 0.1875
Outputs:
- predicted_outcome: bfloat16 [192, 2, 96, 512], P('lon', None, 'lat')
- initial_field_sensitivity: bfloat16 [192, 2, 96, 512], P('lon', None, 'lat')
The draws below stay inside these ranges and needn't reach their ends.
All inputs are finite; a program needn't handle non-finite values.
Results may differ from the reference program's by a relative error of at most 0.038.
Values may be sent and summed in bfloat16 or wider, within the bound.
No kernel may reach another device: no remote copies, remote signals or barrier semaphores. Data moves between devices by JAX's collectives and lax.ppermute only.
A program may use at most 192 MiB of HBM per device.

```python
import jax
import jax.numpy as jnp
from jax import lax

C0 = 512
C1 = 1024
C2 = 2048
HD = 64
H0 = 8
H1 = 16
H2 = 32
LEV = 2
WLAT = 6
WLON = 12
NLAT = 96
NLON = 192


def projection_draw(key, chan_count, inner_width, strength):
    key_parts = jax.random.split(key, 2)
    scale_in = chan_count ** (-0.5)
    base_draw = jax.random.normal(key_parts[0], (4, chan_count, inner_width), jnp.float32) * scale_in
    common = jax.random.normal(key_parts[1], (chan_count, inner_width), jnp.float32) * (scale_in * strength)
    base_draw = base_draw.at[0].add(common).at[1].add(common)
    return jnp.clip(base_draw, -8.0, 8.0).astype(jnp.bfloat16)


def draw_first_proj(key, part):
    key = jax.random.fold_in(key, 11)
    return projection_draw(key, C0, H0 * HD, 0.0)


def draw_middle_proj(key, part):
    key = jax.random.fold_in(key, 12)
    return projection_draw(key, C1, H1 * HD, 0.0)


def draw_coarse_proj(key, part):
    key = jax.random.fold_in(key, 13)
    return projection_draw(key, C2, H2 * HD, 0.0)


def steps_of(rng, dims, pieces, low, largest):
    loudness, own = 1.0, jax.random.fold_in(rng, 6)
    for position, parts in pieces:
        heights = jnp.exp(jax.random.uniform(jax.random.fold_in(own, position), (parts,), jnp.float32, low / len(pieces), largest / len(pieces)))
        loudness = loudness * jnp.repeat(heights, dims[position] // parts).reshape([-1 if axis == position else 1 for axis in range(len(dims))])
    return loudness


def normal_values(key, shape, width, bound, pieces=(), held_as=jnp.bfloat16):
    drawn = width * jax.random.normal(key, shape, jnp.float32)
    if pieces:
        drawn = drawn * steps_of(key, shape, pieces, -0.22, 0.18)
    return jnp.clip(drawn, -bound, bound).astype(held_as)


def setup_inputs(seed: int = 0) -> dict:
    keys = jax.random.split(jax.random.key(seed), 17)
    return {
        "latent_field": normal_values(keys[0], (NLON, LEV, NLAT, C0), 1.0, 6.0, ((0, 16), (2, 8))),
        "sensitivity": normal_values(keys[1], (NLON, LEV, NLAT, C0), 1.0, 6.0, ((0, 16), (2, 8))),
        "first_gain": jnp.clip(1.0 + 0.18 * jax.random.normal(keys[2], (C0,), jnp.float32), 0.1, 1.9),
        "first_proj": draw_first_proj(jax.random.fold_in(keys[16], 71), 0),
        "merge_gain": jnp.clip(1.0 + 0.18 * jax.random.normal(keys[4], (4 * C0,), jnp.float32), 0.1, 1.9),
        "merge_weight": normal_values(keys[5], (4 * C0, C1), (4 * C0) ** -0.5, 0.125),
        "middle_gain": jnp.clip(1.0 + 0.18 * jax.random.normal(keys[6], (C1,), jnp.float32), 0.1, 1.9),
        "middle_proj": draw_middle_proj(jax.random.fold_in(keys[16], 71), 0),
        "reduce_gain": jnp.clip(1.0 + 0.18 * jax.random.normal(keys[8], (4 * C1,), jnp.float32), 0.1, 1.9),
        "reduce_weight": normal_values(keys[9], (4 * C1, C2), (4 * C1) ** -0.5, 0.09375, ((1, 16),)),
        "coarse_gain": jnp.clip(1.0 + 0.18 * jax.random.normal(keys[10], (C2,), jnp.float32), 0.1, 1.9),
        "coarse_proj": draw_coarse_proj(jax.random.fold_in(keys[16], 71), 0),
        "lift_gain": jnp.clip(1.0 + 0.18 * jax.random.normal(keys[12], (C2,), jnp.float32), 0.1, 1.9),
        "lift_weight": normal_values(keys[13], (C2, 4 * C1), C2 ** -0.5, 0.125, ((1, 16),)),
        "widen_gain": jnp.clip(1.0 + 0.18 * jax.random.normal(keys[14], (C1,), jnp.float32), 0.1, 1.9),
        "widen_weight": normal_values(keys[15], (C1, 4 * C0), C1 ** -0.5, 0.1875),
    }


EPSILON = 1e-05

def quantized_numbers(array_in):
    return lax.optimization_barrier(array_in.astype(jnp.bfloat16))

def product(pattern, first_op, second_op):
    return jnp.einsum(pattern, first_op.astype(jnp.float32), second_op.astype(jnp.float32), precision=lax.Precision.HIGHEST)

def layer_norm(values, gain_vec):
    row_mean = lax.optimization_barrier(jnp.mean(values, axis=-1, keepdims=True))
    centred = values - row_mean
    spread = lax.optimization_barrier(jnp.mean(centred * centred, axis=-1, keepdims=True))
    return centred * lax.rsqrt(spread + EPSILON) * gain_vec

def merge_tokens(values):
    col_count, levels, row_count, chan_count = values.shape
    shaped = values.reshape(col_count // 2, 2, levels, row_count // 2, 2, chan_count)
    return shaped.transpose(0, 2, 3, 4, 1, 5).reshape(col_count // 2, levels, row_count // 2, 4 * chan_count)

def split_tokens(values):
    col_count, levels, row_count, wide_count = values.shape
    shaped = values.reshape(col_count, levels, row_count, 2, 2, wide_count // 4)
    return shaped.transpose(0, 4, 1, 2, 3, 5).reshape(2 * col_count, levels, 2 * row_count, wide_count // 4)

def to_windows(values):
    col_count, levels, row_count, count_of_heads, head_width = values.shape
    shaped = values.reshape(col_count // WLON, WLON, levels, row_count // WLAT, WLAT, count_of_heads, head_width)
    shaped = shaped.transpose(0, 3, 1, 2, 4, 5, 6)
    return shaped.reshape(-1, WLON * levels * WLAT, count_of_heads, head_width)

def from_windows(values, head_shape):
    col_count, levels, row_count, count_of_heads, head_width = head_shape
    shaped = values.reshape(col_count // WLON, row_count // WLAT, WLON, levels, WLAT, count_of_heads, head_width)
    return shaped.transpose(0, 2, 3, 1, 4, 5, 6).reshape(head_shape)

def window_mix(packed, offset):
    inner_width = packed.shape[-1] // 3
    rolled = jnp.roll(packed, -offset, axis=0)
    head_shape = rolled.shape[:3] + (inner_width // HD, HD)
    queries = to_windows(rolled[..., :inner_width].reshape(head_shape))
    keys_win = to_windows(rolled[..., inner_width:2 * inner_width].reshape(head_shape))
    values_win = to_windows(rolled[..., 2 * inner_width:].reshape(head_shape))
    scores = product('wqhe,wkhe->whqk', queries, keys_win) * HD ** (-0.5)
    row_peak = lax.optimization_barrier(jnp.max(scores, axis=-1, keepdims=True))
    weights = jnp.exp(scores - row_peak)
    weights = quantized_numbers(weights / lax.optimization_barrier(jnp.sum(weights, axis=-1, keepdims=True)))
    mixed_out = quantized_numbers(product('whqk,wkhe->wqhe', weights, values_win))
    unrolled = jnp.roll(from_windows(mixed_out, head_shape), offset, axis=0)
    return unrolled.reshape(head_shape[:3] + (inner_width,))

def project_qkv(normed, projection):
    full_proj = product('clrd,tde->clrte', normed, projection[:3])
    return quantized_numbers(full_proj.reshape(full_proj.shape[:3] + (-1,)))

def attention_block(values32, gain_vec, projection, offset):
    normed = quantized_numbers(layer_norm(values32, gain_vec))
    mixed_out = window_mix(project_qkv(normed, projection), offset)
    return quantized_numbers(values32 + product('clre,de->clrd', mixed_out, projection[3]))

def shrink(values32, gain_vec, weight):
    normed = quantized_numbers(layer_norm(merge_tokens(values32), gain_vec))
    return quantized_numbers(product('clrd,de->clre', normed, weight))

def widen_map(values32, gain_vec, weight):
    normed = quantized_numbers(layer_norm(values32, gain_vec))
    return product('clrd,de->clre', normed, weight)

def reference(latent_field, sensitivity, first_gain, first_proj, merge_gain, merge_weight, middle_gain, middle_proj, reduce_gain, reduce_weight, coarse_gain, coarse_proj, lift_gain, lift_weight, widen_gain, widen_weight):
    half_window = WLON // 2

    def evaluate_network(state_in):
        first_f32 = state_in.astype(jnp.float32)
        fine_out = attention_block(first_f32, first_gain, first_proj, half_window)
        sharpest_single_precision = fine_out.astype(jnp.float32)
        middle_in = shrink(sharpest_single_precision, merge_gain, merge_weight)
        middle_out = attention_block(middle_in.astype(jnp.float32), middle_gain, middle_proj, half_window)
        middle_f32 = middle_out.astype(jnp.float32)
        coarse_in = shrink(middle_f32, reduce_gain, reduce_weight)
        coarse_out = attention_block(coarse_in.astype(jnp.float32), coarse_gain, coarse_proj, half_window)
        lifted = quantized_numbers(split_tokens(widen_map(coarse_out.astype(jnp.float32), lift_gain, lift_weight)))
        joined = quantized_numbers(middle_f32 + lifted.astype(jnp.float32))
        broadened_patches = split_tokens(widen_map(joined.astype(jnp.float32), widen_gain, widen_weight))
        return quantized_numbers(sharpest_single_precision + broadened_patches)
    predicted_outcome, undo_placement = jax.vjp(evaluate_network, latent_field)
    initial_field_sensitivity, = undo_placement(sensitivity)
    return (predicted_outcome, initial_field_sensitivity)
```

```python
import functools

import jax
import jax.numpy as jnp
import numpy as np
from jax import lax
from jax.experimental import pallas as pl
from jax.experimental.pallas import tpu as pltpu
from jax.sharding import PartitionSpec as P

BF = jnp.bfloat16
F32 = jnp.float32
EPSILON = 1e-05
HD = 64
GROUP = 4 * HD
LAT, LON = 8, 16
AXES = ("lat", "lon")
T0, T1, T2 = 288, 72, 18
PAD = 24
C0, C1, C2 = 512, 1024, 2048
MIB = 1024 * 1024


def orders():
    window, merge = {}, {}
    for c in range(12):
        for lev in range(2):
            for r in range(12):
                nat = (c * 2 + lev) * 12 + r
                cw, ci, b = c // 6, c % 6 // 2, c % 2
                rw, rj, a = r // 6, r % 6 // 2, r % 2
                s = 2 * a + b
                window[nat] = (cw * 2 + rw) * 72 + s * 18 + (ci * 2 + lev) * 3 + rj
                mc, mr = c // 2, r // 2
                s1 = 2 * (mr % 2) + mc % 2
                merge[nat] = s * 72 + s1 * 18 + (mc // 2 * 2 + lev) * 3 + mr // 2
    to_window = np.zeros((T0, T0), np.float32)
    to_merge = np.zeros((T0, T0), np.float32)
    for nat in range(T0):
        to_window[window[nat], nat] = 1
        to_merge[merge[nat], nat] = 1
    half = np.zeros((144, 144), np.float32)
    for nat in range(144):
        half[window[nat], nat] = 1
    return to_window, half, to_merge


TO_WINDOW, HALF_WINDOW, TO_MERGE = orders()
WINDOW_TO_MERGE = TO_MERGE @ TO_WINDOW.T


def number(lat, lon):
    return lat % LAT * LON + lon % LON


def member_pairs(mask):
    pairs = []
    for lat in range(LAT):
        for lon in range(LON):
            other = ((lon - 2) % LON) ^ (mask & 3)
            pairs.append((number(lat, lon), number(lat ^ (mask >> 2), other + 2)))
    return pairs


def lon_pairs(shift):
    return [(number(a, i), number(a, i + shift)) for a in range(LAT) for i in range(LON)]


def half_pairs():
    return [
        (number(a, i), number(a, i + 1 if i % 2 else i - 1)) for a in range(LAT) for i in range(LON)
    ]


def send(value, pairs):
    return lax.ppermute(value, AXES, pairs)


def gather8(block):
    chips = jnp.stack([block] + [send(block, member_pairs(mask)) for mask in (2, 4, 6)])
    return chips, send(chips, member_pairs(1))


def scatter8(even, odd):
    both = (even.astype(F32) + send(odd, member_pairs(1)).astype(F32)).astype(BF)
    return [both[0]] + [send(both[j], member_pairs(2 * j)) for j in (1, 2, 3)]


def exchange8(even, odd):
    both = jnp.stack([even, send(odd, member_pairs(1))], axis=1)
    return [both[0]] + [send(both[j], member_pairs(2 * j)) for j in (1, 2, 3)]


def nn(a, b):
    return lax.dot_general(
        a.astype(BF), b.astype(BF), (((1,), (0,)), ((), ())), preferred_element_type=F32
    )


def nt(a, b):
    return lax.dot_general(
        a.astype(BF), b.astype(BF), (((1,), (1,)), ((), ())), preferred_element_type=F32
    )


def tn(a, b):
    return lax.dot_general(
        a.astype(BF), b.astype(BF), (((0,), (0,)), ((), ())), preferred_element_type=F32
    )


def rounded(value):
    return value.astype(BF).astype(F32)


def norm_parts(pieces):
    width = sum(v.shape[1] for v in pieces)
    mean = sum(jnp.sum(v, axis=1, keepdims=True) for v in pieces) / width
    centred = [v - mean for v in pieces]
    spread = sum(jnp.sum(v * v, axis=1, keepdims=True) for v in centred) / width
    scale = lax.rsqrt(spread + EPSILON)
    return [v * scale for v in centred], scale


def norm_back(unit, scale, cot):
    width = sum(v.shape[1] for v in unit)
    first = sum(jnp.sum(v, axis=1, keepdims=True) for v in cot) / width
    second = sum(jnp.sum(v * u, axis=1, keepdims=True) for v, u in zip(cot, unit)) / width
    return [scale * (v - first - u * second) for v, u in zip(cot, unit)]


def head_masks():
    lane = lax.broadcasted_iota(jnp.int32, (1, GROUP), 1) // HD
    return [(lane == h).astype(F32) for h in range(4)]


def by_head(value):
    return jnp.concatenate([value * m for m in head_masks()], axis=0)


def own_heads(value, rows):
    return sum(value[h * rows : (h + 1) * rows] * m for h, m in enumerate(head_masks()))


def weights_of(q, k, dead):
    scores = nt(by_head(q), k) * HD ** (-0.5)
    if dead is not None:
        scores = jnp.where(dead, -1e30, scores)
    raised = jnp.exp(scores - jnp.max(scores, axis=1, keepdims=True))
    return raised / jnp.sum(raised, axis=1, keepdims=True)


def mix(q, k, v, dead=None):
    return rounded(own_heads(nn(weights_of(q, k, dead), v), q.shape[0]))


def mix_back(q, k, v, grad, dead=None):
    rows = q.shape[0]
    weights = weights_of(q, k, dead)
    grads = by_head(grad)
    from_weights = nt(grads, v)
    inner = jnp.sum(weights * from_weights, axis=1, keepdims=True)
    from_scores = weights * (from_weights - inner) * HD ** (-0.5)
    return (
        rounded(own_heads(nn(from_scores, k), rows)),
        rounded(tn(from_scores, by_head(q))),
        rounded(tn(weights, grads)),
    )


def call(body, outs, args, scalars=0, scratch=(), flops=0):
    specs = [pl.BlockSpec(memory_space=pltpu.SMEM)] * scalars
    specs += [pl.BlockSpec(memory_space=pltpu.VMEM)] * (len(args) - scalars)
    moved = sum(int(np.prod(a.shape)) * a.dtype.itemsize for a in args)
    return pl.pallas_call(
        body,
        out_shape=[jax.ShapeDtypeStruct(shape, dtype) for shape, dtype in outs],
        in_specs=specs,
        out_specs=[pl.BlockSpec(memory_space=pltpu.VMEM)] * len(outs),
        scratch_shapes=list(scratch),
        compiler_params=pltpu.CompilerParams(vmem_limit_bytes=48 * MIB),
        cost_estimate=pl.CostEstimate(flops=flops, bytes_accessed=moved, transcendentals=0),
    )(*args)


def half_pick(which, rows, columns):
    row = lax.broadcasted_iota(jnp.int32, (rows, columns), 0)
    column = lax.broadcasted_iota(jnp.int32, (rows, columns), 1)
    return (column == row + which * rows).astype(BF)


def member_rows(read, member):
    q, p = member % 4, member // 4
    return jnp.concatenate([read((4 * z + q) * 128 + p * 64) for z in range(4)], axis=0)


def turn_middle(w, out):
    pick = half_pick(0, 64, 64)
    for t in range(4):
        out[t] = nt(pick, w[t]).astype(BF)


def turn_reduce(where, w, out):
    pick = half_pick(where[1], 64, 128)
    for j in range(8):
        out[:, j * 512 : (j + 1) * 512] = nt(pick, w[j * 512 : (j + 1) * 512]).astype(BF)


def turn_coarse(where, w, out):
    pick = half_pick(where[1], 64, 128)
    for t in range(4):
        for a in range(8):
            rows = member_rows(lambda at: w[t, at : at + 64], a)
            out[t, :, a * 256 : (a + 1) * 256] = nt(pick, rows).astype(BF)


def turn_lift(where, w, out):
    pick = half_pick(where[1], 128, 256)
    for a in range(8):
        rows = member_rows(lambda at: w[at : at + 64], a)
        out[:, a * 256 : (a + 1) * 256] = nt(pick, rows).astype(BF)


def fine_forward(x, left, right, to_window, half, to_merge, gain, w, mgain, mw, fine, mid, own, far):
    xo = nn(to_window[...], x[...])
    xh = jnp.concatenate([nn(half[...], left[...]), nn(half[...], right[...])], axis=0)
    packs = []
    for value, kept in ((xo, own), (xh, far)):
        (unit,), _ = norm_parts([value])
        normed = (unit * gain[...]).astype(BF)
        pack = [rounded(nn(normed, w[t])) for t in range(3)]
        for t in range(3):
            kept[t] = pack[t].astype(BF)
        packs.append(pack)
    rows = []
    for at in range(0, T0, 72):
        parts = []
        for ch in range(0, C0, GROUP):
            q = packs[0][0][at : at + 72, ch : ch + GROUP]
            k, v = [
                jnp.concatenate([pk[t][at : at + 72, ch : ch + GROUP] for pk in packs], axis=0)
                for t in (1, 2)
            ]
            parts.append(mix(q, k, v))
        rows.append(jnp.concatenate(parts, axis=1))
    mixed = jnp.concatenate(rows, axis=0)
    out = rounded(xo + nt(mixed, w[3]))
    merged = nn(to_merge[...], out)
    fine[...] = merged.astype(BF)
    units, _ = norm_parts([merged[s * 72 : (s + 1) * 72] for s in range(4)])
    total = 0.0
    for s in range(4):
        span = slice(s * C0, (s + 1) * C0)
        total = total + nn(units[s] * mgain[:, span], mw[span])
    mid[...] = total.astype(BF)


def heads_of(w, g, t):
    return jnp.concatenate([w[4 * g + h, t] for h in range(4)], axis=0)


def middle_forward(x, partner, gain, w, rgain, out, packed, reduced, buf):
    own = x[...].astype(F32)
    both = jnp.concatenate([own, partner[...].astype(F32)], axis=0)
    (unit,), _ = norm_parts([both])
    normed = (unit * gain[...]).astype(BF)
    total = own
    for g in range(4):
        span = slice(g * GROUP, (g + 1) * GROUP)
        pack = [rounded(nt(normed, heads_of(w, g, t))) for t in range(3)]
        for t in range(3):
            packed[t, :, span] = pack[t].astype(BF)
        total = total + nn(mix(pack[0][:T1], pack[1], pack[2]), heads_of(w, g, 3))
    out[...] = total.astype(BF)
    buf[...] = rounded(total)
    units, _ = norm_parts([buf[s * T2 : (s + 1) * T2] for s in range(4)])
    for s in range(4):
        span = slice(s * C1, (s + 1) * C1)
        reduced[:, span] = (units[s] * rgain[:, span]).astype(BF)


def tokens_into(buf, blocks):
    buf[...] = jnp.zeros_like(buf)
    for k, block in enumerate(blocks):
        buf[k * PAD : k * PAD + T2] = block.astype(F32)


def paired(chips, mates):
    return [(chips, mates)[k % 2][k // 2] for k in range(8)]


def blocks_out(value, even, odd):
    for k in range(8):
        (even, odd)[k % 2][k // 2] = value[k * PAD : k * PAD + T2].astype(BF)


def coarse_reduce(chips, mates, w, out, buf):
    tokens_into(buf, paired(chips, mates))
    columns = nt(buf[...], jnp.concatenate([w[z] for z in range(4)], axis=0))
    for k in range(8):
        out[k] = columns[k * PAD : k * PAD + T2].astype(BF)


def dead_keys():
    return lax.broadcasted_iota(jnp.int32, (1, 8 * PAD), 1) % PAD >= T2


def coarse_heads(w, t):
    return jnp.concatenate([w[z, t] for z in range(4)], axis=0)


def coarse_forward(where, chips, mates, gain, w, even, odd, packed, kept, buf):
    me = where[0]
    buf[...] = jnp.zeros_like(buf)
    for j in range(8):
        source = (chips, mates)[j % 2]
        for k in range(8):
            at = (k ^ j) * PAD
            buf[me ^ j, at : at + T2] = source[j // 2, k].astype(F32)
    units, _ = norm_parts([buf[a] for a in range(8)])
    for a in range(8):
        kept[:, a * 256 : (a + 1) * 256] = buf[a, :T2].astype(BF)
    normed = jnp.concatenate(
        [(units[a] * gain[:, a * 256 : (a + 1) * 256]).astype(BF) for a in range(8)], axis=1
    )
    pack = [rounded(nt(normed, coarse_heads(w, t))) for t in range(3)]
    for t in range(3):
        packed[t] = pack[t].astype(BF)
    mixed = mix(pack[0], pack[1], pack[2], dead_keys())
    blocks_out(nn(mixed, coarse_heads(w, 3)), even, odd)


def total_of(parts):
    return sum(p[...].astype(F32) for p in parts)


def coarse_finish(a, b, c, d, x, gain, out, normed):
    value = rounded(x[...].astype(F32) + total_of((a, b, c, d)))
    out[...] = value.astype(BF)
    (unit,), _ = norm_parts([value])
    normed[...] = (unit * gain[...]).astype(BF)


def lift_forward(chips, mates, w, even, odd, buf):
    tokens_into(buf, paired(chips, mates))
    blocks_out(nt(buf[...], jnp.concatenate([w[z] for z in range(4)], axis=0)), even, odd)


def sens_back(sens, to_merge, ww, merged, grad):
    value = nn(to_merge[...], sens[...])
    merged[...] = value.astype(BF)
    total = 0.0
    for s in range(4):
        total = total + nt(value[s * 72 : (s + 1) * 72], ww[:, s * C0 : (s + 1) * C0])
    grad[...] = total.astype(BF)


def member_lanes(me, k):
    member = me ^ k
    return pl.multiple_of((member % 4) * 256 + member // 4 * 128, 128)


def turn_point(
    where, a, b, c, d, mid, fine, grad, gain, ww, to_nat, out, joined_grad, even, odd, wide, flat
):
    me = where[0]
    for j, source in enumerate((a, b, c, d)):
        for i in range(2):
            at = member_lanes(me, 2 * j + i)
            block = source[i].astype(F32)
            for s in range(4):
                wide[s, :, pl.ds(at, 128)] = block[:, s * 128 : (s + 1) * 128]
    for s in range(4):
        flat[s * T2 : (s + 1) * T2] = wide[s]
    joined = rounded(mid[...].astype(F32) + flat[...])
    (unit,), scale = norm_parts([joined])
    normed = (unit * gain[...]).astype(BF)
    rows = [
        fine[s * 72 : (s + 1) * 72].astype(F32) + nn(normed, ww[:, s * C0 : (s + 1) * C0])
        for s in range(4)
    ]
    merged = jnp.concatenate(rows, axis=0)
    out[...] = lax.dot_general(
        to_nat[...], merged.astype(BF), (((1,), (0,)), ((), ())), preferred_element_type=F32
    ).astype(BF)
    (back,) = norm_back([unit], scale, [grad[...].astype(F32) * gain[...]])
    joined_grad[...] = back.astype(BF)
    flat[...] = rounded(back)
    for s in range(4):
        wide[s] = flat[s * T2 : (s + 1) * T2]
    for k in range(8):
        at = member_lanes(me, k)
        for s in range(4):
            (even, odd)[k % 2][k // 2, :, s * 128 : (s + 1) * 128] = wide[s, :, pl.ds(at, 128)].astype(
                BF
            )


def from_chips(parts):
    return [parts[k // 2][k % 2] for k in range(8)]


def lift_back(a, b, c, d, w, even, odd, buf):
    tokens_into(buf, from_chips((a, b, c, d)))
    blocks_out(nn(buf[...], jnp.concatenate([w[z] for z in range(4)], axis=0)), even, odd)


def coarse_out_back(a, b, c, d, value, gain, out):
    (unit,), scale = norm_parts([value[...].astype(F32)])
    cot = rounded(total_of((a, b, c, d))) * gain[...]
    out[...] = norm_back([unit], scale, [cot])[0].astype(BF)


def coarse_back(chips, mates, packed, w, even, odd, buf):
    tokens_into(buf, paired(chips, mates))
    grad = rounded(nt(buf[...], coarse_heads(w, 3)))
    pack = [packed[t].astype(F32) for t in range(3)]
    grads = mix_back(pack[0], pack[1], pack[2], grad, dead_keys())
    blocks_out(sum(nn(grads[t], coarse_heads(w, t)) for t in range(3)), even, odd)


def coarse_in_back(where, a, b, c, d, value, gain, grad, even, odd, buf):
    me = where[0]
    (unit,), scale = norm_parts([value[...].astype(F32)])
    cot = rounded(total_of((a, b, c, d))) * gain[...]
    buf[...] = grad[...].astype(F32) + norm_back([unit], scale, [cot])[0]
    for k in range(8):
        at = pl.multiple_of((me ^ k) * 256, 256)
        (even, odd)[k % 2][k // 2] = buf[:, pl.ds(at, 256)].astype(BF)


def reduce_back(a, b, c, d, w, even, odd, buf):
    tokens_into(buf, from_chips((a, b, c, d)))
    blocks_out(nn(buf[...], jnp.concatenate([w[z] for z in range(4)], axis=0)), even, odd)


def middle_out_back(a, b, c, d, mid, gain, grad, out, buf, back):
    buf[...] = mid[...].astype(F32)
    units, scale = norm_parts([buf[s * T2 : (s + 1) * T2] for s in range(4)])
    cot = rounded(total_of((a, b, c, d))) * gain[...]
    backs = norm_back(units, scale, [cot[:, s * C1 : (s + 1) * C1] for s in range(4)])
    for s in range(4):
        back[s * T2 : (s + 1) * T2] = backs[s]
    out[...] = (grad[...].astype(F32) + back[...]).astype(BF)


def middle_back(grad, partner, x, packed, gain, w, fine, sens, mgain, mw, to_window, out):
    own = grad[...].astype(F32)
    both = jnp.concatenate([own, partner[...].astype(F32)], axis=0)
    total = 0.0
    for g in range(4):
        span = slice(g * GROUP, (g + 1) * GROUP)
        mixed = rounded(nt(both, heads_of(w, g, 3)))
        pack = [packed[t, :, span].astype(F32) for t in range(3)]
        grads = mix_back(pack[0], pack[1], pack[2], mixed)
        for t in range(3):
            total = total + nn(grads[t][:T1], heads_of(w, g, t))
    (unit,), scale = norm_parts([x[...].astype(F32)])
    into = (own + norm_back([unit], scale, [rounded(total) * gain[...]])[0]).astype(BF)
    units, scale = norm_parts([fine[s * 72 : (s + 1) * 72].astype(F32) for s in range(4)])
    cots = []
    for s in range(4):
        span = slice(s * C0, (s + 1) * C0)
        cots.append(rounded(nt(into, mw[span])) * mgain[:, span])
    backs = jnp.concatenate(norm_back(units, scale, cots), axis=0)
    out[...] = nn(to_window[...], sens[...].astype(F32) + backs).astype(BF)


def fine_back(grad, left, right, own, far, x, to_window, to_nat, gain, w, out):
    go = grad[...]
    mixed_own = rounded(nn(go, w[3]))
    mixed_far = jnp.concatenate([rounded(nn(v[...], w[3])) for v in (left, right)], axis=0)
    rows = [[], [], []]
    for at in range(0, T0, 72):
        parts = [[], [], []]
        for ch in range(0, C0, GROUP):
            span, lanes = slice(at, at + 72), slice(ch, ch + GROUP)
            pack = [
                jnp.concatenate(
                    [own[t, span, lanes].astype(F32), far[t, span, lanes].astype(F32)], axis=0
                )
                for t in range(3)
            ]
            mixed = jnp.concatenate([mixed_own[span, lanes], mixed_far[span, lanes]], axis=0)
            grads = mix_back(pack[0], pack[1], pack[2], mixed)
            for t in range(3):
                parts[t].append(grads[t][:72])
        for t in range(3):
            rows[t].append(jnp.concatenate(parts[t], axis=1))
    total = sum(nt(jnp.concatenate(rows[t], axis=0), w[t]) for t in range(3))
    (unit,), scale = norm_parts([nn(to_window[...], x[...])])
    back = go.astype(F32) + norm_back([unit], scale, [rounded(total) * gain[...]])[0]
    out[...] = nn(to_nat[...], back).astype(BF)


def local(
    latent_field,
    sensitivity,
    first_gain,
    first_proj,
    merge_gain,
    merge_weight,
    middle_gain,
    middle_proj,
    reduce_gain,
    reduce_weight,
    coarse_gain,
    coarse_proj,
    lift_gain,
    lift_weight,
    widen_gain,
    widen_weight,
):
    lat, lon = lax.axis_index("lat"), lax.axis_index("lon")
    where = jnp.stack([lat % 2 * 4 + lon % 4, lat % 2]).astype(jnp.int32)
    columns = [[q + 4 * z for z in range(4)] for q in range(4)]

    def row(gain):
        return gain.reshape(1, -1)

    def member_row(gain):
        return gain.reshape(4, 4, 2, 64).transpose(2, 1, 0, 3).reshape(1, -1)

    def over_z(value):
        return lax.all_gather(value, "lon", axis_index_groups=columns, axis=0)

    to_window = jnp.asarray(TO_WINDOW, BF)
    from_window = jnp.asarray(TO_WINDOW.T, BF)
    half = jnp.asarray(HALF_WINDOW, BF)
    to_merge = jnp.asarray(TO_MERGE, BF)
    from_merge = jnp.asarray(TO_MERGE.T, BF)
    window_to_merge = jnp.asarray(WINDOW_TO_MERGE, BF)
    merge_to_window = jnp.asarray(WINDOW_TO_MERGE.T, BF)

    (mid_part,) = call(turn_middle, [((4, 64, C1), BF)], (middle_proj,))
    mid_w = lax.all_gather(mid_part, "lon", axis=0)
    (reduce_part,) = call(turn_reduce, [((64, 4 * C1), BF)], (where, reduce_weight), 1)
    reduce_w = over_z(reduce_part)
    (coarse_part,) = call(turn_coarse, [((4, 64, C2), BF)], (where, coarse_proj), 1)
    coarse_w = over_z(coarse_part)
    (lift_part,) = call(turn_lift, [((128, C2), BF)], (where, lift_weight), 1)
    lift_w = over_z(lift_part)

    x = latent_field.reshape(T0, C0)
    from_left = send(x[144:], lon_pairs(1))
    from_right = send(x[:144], lon_pairs(-1))
    fine, mid_in, own, far = call(
        fine_forward,
        [((T0, C0), BF), ((T1, C1), BF), ((3, T0, C0), BF), ((3, T0, C0), BF)],
        (x, from_left, from_right, to_window, half, window_to_merge, row(first_gain), first_proj,
         row(merge_gain), merge_weight),
    )
    sens, sens_grad = call(
        sens_back,
        [((T0, C0), BF), ((T1, C1), BF)],
        (sensitivity.reshape(T0, C0), to_merge, widen_weight),
    )
    mid_far = send(mid_in, half_pairs())
    mid, mid_packed, reduced = call(
        middle_forward,
        [((T1, C1), BF), ((3, 2 * T1, C1), BF), ((T2, 4 * C1), BF)],
        (mid_in, mid_far, row(middle_gain), mid_w, row(reduce_gain)),
        scratch=[pltpu.VMEM((T1, C1), F32)],
    )
    rows = 8 * PAD
    (columns_in,) = call(
        coarse_reduce,
        [((8, T2, 256), BF)],
        (*gather8(reduced), reduce_w),
        scratch=[pltpu.VMEM((rows, 4 * C1), F32)],
    )

    def halves(width):
        return [((4, T2, width), BF), ((4, T2, width), BF)]

    even, odd, coarse_packed, coarse_in = call(
        coarse_forward,
        halves(C2) + [((3, rows, 256), BF), ((T2, C2), BF)],
        (where, *gather8(columns_in), member_row(coarse_gain), coarse_w),
        1,
        scratch=[pltpu.VMEM((8, rows, 256), F32)],
    )
    coarse_out, lift_in = call(
        coarse_finish,
        [((T2, C2), BF), ((T2, C2), BF)],
        (*scatter8(even, odd), coarse_in, member_row(lift_gain)),
    )
    even, odd = call(
        lift_forward,
        halves(512),
        (*gather8(lift_in), lift_w),
        scratch=[pltpu.VMEM((rows, C2), F32)],
    )
    predicted, joined_grad, even, odd = call(
        turn_point,
        [((T0, C0), BF), ((T1, C1), BF)] + halves(512),
        (where, *exchange8(even, odd), mid, fine, sens_grad, row(widen_gain), widen_weight, from_merge),
        1,
        scratch=[pltpu.VMEM((4, T2, C1), F32), pltpu.VMEM((T1, C1), F32)],
    )
    even, odd = call(
        lift_back,
        halves(C2),
        (*exchange8(even, odd), lift_w),
        scratch=[pltpu.VMEM((rows, 512), F32)],
    )
    (coarse_grad,) = call(
        coarse_out_back,
        [((T2, C2), BF)],
        (*scatter8(even, odd), coarse_out, member_row(lift_gain)),
    )
    even, odd = call(
        coarse_back,
        halves(C2),
        (*gather8(coarse_grad), coarse_packed, coarse_w),
        scratch=[pltpu.VMEM((rows, C2), F32)],
    )
    even, odd = call(
        coarse_in_back,
        halves(256),
        (where, *scatter8(even, odd), coarse_in, member_row(coarse_gain), coarse_grad),
        1,
        scratch=[pltpu.VMEM((T2, C2), F32)],
    )
    even, odd = call(
        reduce_back,
        halves(4 * C1),
        (*exchange8(even, odd), reduce_w),
        scratch=[pltpu.VMEM((rows, 256), F32)],
    )
    (mid_grad,) = call(
        middle_out_back,
        [((T1, C1), BF)],
        (*scatter8(even, odd), mid, row(reduce_gain), joined_grad),
        scratch=[pltpu.VMEM((T1, C1), F32), pltpu.VMEM((T1, C1), F32)],
    )
    (fine_grad,) = call(
        middle_back,
        [((T0, C0), BF)],
        (mid_grad, send(mid_grad, half_pairs()), mid_in, mid_packed, row(middle_gain), mid_w, fine,
         sens, row(merge_gain), merge_weight, merge_to_window),
    )
    grad_left = send(fine_grad[144:], lon_pairs(1))
    grad_right = send(fine_grad[:144], lon_pairs(-1))
    (result,) = call(
        fine_back,
        [((T0, C0), BF)],
        (fine_grad, grad_left, grad_right, own, far, x, to_window, from_window, row(first_gain),
         first_proj),
    )
    shape = latent_field.shape
    return predicted.reshape(shape), result.reshape(shape)


def solution(mesh):
    field = P("lon", None, "lat", None)
    placed = (
        field, field, P(), P(), P(), P(), P(), P(None, None, "lon"), P(), P(None, "lon"), P(),
        P(None, None, "lon"), P(), P(None, "lon"), P(), P(),
    )
    return jax.shard_map(
        local, mesh=mesh, in_specs=placed, out_specs=(field, field), check_vma=False
    )
```

```python
import functools

import jax
import jax.numpy as jnp
import numpy as np
from jax import lax
from jax.experimental import pallas as pl
from jax.experimental.pallas import tpu as pltpu
from jax.sharding import PartitionSpec as P

BF = jnp.bfloat16
F32 = jnp.float32
EPSILON = 1e-05
HD = 64
GROUP = 4 * HD
LAT, LON = 8, 16
AXES = ("lat", "lon")
T0, T1, T2 = 288, 72, 18
PAD = 24
C0, C1, C2 = 512, 1024, 2048
MIB = 1024 * 1024


def orders():
    window, merge = {}, {}
    for c in range(12):
        for lev in range(2):
            for r in range(12):
                nat = (c * 12 + r) * 2 + lev
                cw, ci, b = c // 6, c % 6 // 2, c % 2
                rw, rj, a = r // 6, r % 6 // 2, r % 2
                s = 2 * a + b
                window[nat] = (cw * 2 + rw) * 72 + s * 18 + (ci * 2 + lev) * 3 + rj
                mc, mr = c // 2, r // 2
                s1 = 2 * (mr % 2) + mc % 2
                merge[nat] = s * 72 + s1 * 18 + (mc // 2 * 2 + lev) * 3 + mr // 2
    to_window = np.zeros((T0, T0), np.float32)
    to_merge = np.zeros((T0, T0), np.float32)
    for nat in range(T0):
        to_window[window[nat], nat] = 1
        to_merge[merge[nat], nat] = 1
    half = np.zeros((144, 144), np.float32)
    for nat in range(144):
        half[window[nat], nat] = 1
    return to_window, half, to_merge


TO_WINDOW, HALF_WINDOW, TO_MERGE = orders()
WINDOW_TO_MERGE = TO_MERGE @ TO_WINDOW.T


def number(lat, lon):
    return lat % LAT * LON + lon % LON


def pairs_of(rule):
    return [(number(a, i), number(*rule(a, i))) for a in range(LAT) for i in range(LON)]


def member_of(lat, lon, k):
    shifted = (lon - 2) % LON
    window = shifted // 4
    owner = 2 * (lat % 2) + shifted % 4 // 2
    return lat // 2 * 2 + window // 2, 4 * (owner ^ k) + 2 * (window % 2) + lon % 2


OUT = [pairs_of(lambda a, i, k=k: member_of(a, i, k)) for k in range(4)]
BACK = [[(target, source) for source, target in pairs] for pairs in OUT]
RING = [pairs_of(lambda a, i, k=k: (a, i ^ (4 * k))) for k in range(4)]
CORE = pairs_of(lambda a, i: (a, i ^ 1))
NEAR = pairs_of(lambda a, i: (a, i ^ 2))
NEAR_OTHER = pairs_of(lambda a, i: (a ^ 1, i ^ 2))
RIGHT = pairs_of(lambda a, i: (a, i + 1))
LEFT = pairs_of(lambda a, i: (a, i - 1))
HALF = pairs_of(lambda a, i: (a, i + 1 if i % 2 else i - 1))


def send(value, pairs):
    return lax.ppermute(value, AXES, pairs)


def to_ring(block):
    chips = jnp.concatenate([send(block, OUT[k]) for k in range(4)])
    return chips, send(chips, CORE)


def gather8(block):
    chips = jnp.concatenate([block] + [send(block, RING[k]) for k in (1, 2, 3)])
    return chips, send(chips, CORE)


def scatter8(even, odd):
    both = (even.astype(F32) + send(odd, CORE).astype(F32)).astype(BF)
    parts = [both[k * PAD : (k + 1) * PAD] for k in range(4)]
    return [parts[0]] + [send(parts[k], RING[k]) for k in (1, 2, 3)]


def exchange8(even, odd, ways):
    other = send(odd, CORE)
    return [
        send(jnp.concatenate([even[k * PAD : (k + 1) * PAD], other[k * PAD : (k + 1) * PAD]]), ways[k])
        for k in range(4)
    ]


def nn(a, b):
    return lax.dot_general(
        a.astype(BF), b.astype(BF), (((1,), (0,)), ((), ())), preferred_element_type=F32
    )


def nt(a, b):
    return lax.dot_general(
        a.astype(BF), b.astype(BF), (((1,), (1,)), ((), ())), preferred_element_type=F32
    )


def tn(a, b):
    return lax.dot_general(
        a.astype(BF), b.astype(BF), (((0,), (0,)), ((), ())), preferred_element_type=F32
    )


def rounded(value):
    return value.astype(BF).astype(F32)


def norm_parts(pieces):
    width = sum(v.shape[1] for v in pieces)
    mean = sum(jnp.sum(v, axis=1, keepdims=True) for v in pieces) / width
    centred = [v - mean for v in pieces]
    spread = sum(jnp.sum(v * v, axis=1, keepdims=True) for v in centred) / width
    scale = lax.rsqrt(spread + EPSILON)
    return [v * scale for v in centred], scale


def norm_back(unit, scale, cot):
    width = sum(v.shape[1] for v in unit)
    first = sum(jnp.sum(v, axis=1, keepdims=True) for v in cot) / width
    second = sum(jnp.sum(v * u, axis=1, keepdims=True) for v, u in zip(cot, unit)) / width
    return [scale * (v - first - u * second) for v, u in zip(cot, unit)]


def head_masks():
    lane = lax.broadcasted_iota(jnp.int32, (1, GROUP), 1) // HD
    return [(lane == h).astype(F32) for h in range(4)]


def by_head(value):
    return jnp.concatenate([value * m for m in head_masks()], axis=0)


def own_heads(value, rows):
    return sum(value[h * rows : (h + 1) * rows] * m for h, m in enumerate(head_masks()))


def weights_of(q, k, dead):
    scores = nt(by_head(q), k) * HD ** (-0.5)
    if dead is not None:
        scores = jnp.where(dead, -1e30, scores)
    raised = jnp.exp(scores - jnp.max(scores, axis=1, keepdims=True))
    return raised / jnp.sum(raised, axis=1, keepdims=True)


def mix(q, k, v, dead=None):
    return rounded(own_heads(nn(weights_of(q, k, dead), v), q.shape[0]))


def mix_back(q, k, v, grad, dead=None):
    rows = q.shape[0]
    weights = weights_of(q, k, dead)
    grads = by_head(grad)
    from_weights = nt(grads, v)
    inner = jnp.sum(weights * from_weights, axis=1, keepdims=True)
    from_scores = weights * (from_weights - inner) * HD ** (-0.5)
    return (
        rounded(own_heads(nn(from_scores, k), rows)),
        rounded(tn(from_scores, by_head(q))),
        rounded(tn(weights, grads)),
    )


def call(body, outs, args, scalars=0, scratch=(), vmem=16):
    specs = [pl.BlockSpec(memory_space=pltpu.SMEM)] * scalars
    specs += [pl.BlockSpec(memory_space=pltpu.VMEM)] * (len(args) - scalars)
    moved = sum(int(np.prod(a.shape)) * a.dtype.itemsize for a in args)
    return pl.pallas_call(
        body,
        out_shape=[jax.ShapeDtypeStruct(shape, dtype) for shape, dtype in outs],
        in_specs=specs,
        out_specs=[pl.BlockSpec(memory_space=pltpu.VMEM)] * len(outs),
        scratch_shapes=list(scratch),
        compiler_params=pltpu.CompilerParams(vmem_limit_bytes=vmem * MIB),
        cost_estimate=pl.CostEstimate(flops=0, bytes_accessed=moved, transcendentals=0),
    )(*args)


def fine_forward(x, left, right, to_window, half, to_merge, gain, w, mgain, mw, fine, mid, own, far):
    xo = nn(to_window[...], x[...])
    xh = jnp.concatenate([nn(half[...], left[...]), nn(half[...], right[...])], axis=0)
    packs = []
    for value, kept in ((xo, own), (xh, far)):
        (unit,), _ = norm_parts([value])
        normed = (unit * gain[...]).astype(BF)
        pack = [rounded(nn(normed, w[t])) for t in range(3)]
        for t in range(3):
            kept[t] = pack[t].astype(BF)
        packs.append(pack)
    rows = []
    for at in range(0, T0, 72):
        parts = []
        for ch in range(0, C0, GROUP):
            q = packs[0][0][at : at + 72, ch : ch + GROUP]
            k, v = [
                jnp.concatenate([pk[t][at : at + 72, ch : ch + GROUP] for pk in packs], axis=0)
                for t in (1, 2)
            ]
            parts.append(mix(q, k, v))
        rows.append(jnp.concatenate(parts, axis=1))
    mixed = jnp.concatenate(rows, axis=0)
    out = rounded(xo + nt(mixed, w[3]))
    merged = nn(to_merge[...], out)
    fine[...] = merged.astype(BF)
    units, _ = norm_parts([merged[s * 72 : (s + 1) * 72] for s in range(4)])
    total = 0.0
    for s in range(4):
        span = slice(s * C0, (s + 1) * C0)
        total = total + nn(units[s] * mgain[:, span], mw[span])
    mid[...] = total.astype(BF)


def heads_of(w, g, t):
    return jnp.concatenate([w[4 * g + h, t] for h in range(4)], axis=0)


def middle_forward(x, partner, gain, w, rgain, out, packed, reduced, buf):
    own = x[...].astype(F32)
    both = jnp.concatenate([own, partner[...].astype(F32)], axis=0)
    (unit,), _ = norm_parts([both])
    normed = (unit * gain[...]).astype(BF)
    total = own
    for g in range(4):
        span = slice(g * GROUP, (g + 1) * GROUP)
        pack = [rounded(nt(normed, heads_of(w, g, t))) for t in range(3)]
        for t in range(3):
            packed[t, :, span] = pack[t].astype(BF)
        total = total + nn(mix(pack[0][:T1], pack[1], pack[2]), heads_of(w, g, 3))
    out[...] = total.astype(BF)
    buf[...] = rounded(total)
    units, _ = norm_parts([buf[s * T2 : (s + 1) * T2] for s in range(4)])
    reduced[...] = jnp.zeros_like(reduced)
    for s in range(4):
        span = slice(s * C1, (s + 1) * C1)
        reduced[:T2, span] = (units[s] * rgain[:, span]).astype(BF)


def beside(parts):
    return jnp.concatenate([part[...] for part in parts], axis=1)


def below(parts):
    return jnp.concatenate([part[...] for part in parts], axis=0)


def halves_out(value, even, odd):
    even[...] = value[: 4 * PAD].astype(BF)
    odd[...] = value[4 * PAD :].astype(BF)


def coarse_reduce(chips, mates, own, low, high, out):
    tokens = below((chips, mates))
    out[:, :128] = nn(tokens, own[...]).astype(BF)
    out[:, 128:] = nn(tokens, below((low, high))).astype(BF)


def dead_keys():
    return lax.broadcasted_iota(jnp.int32, (1, 8 * PAD), 1) % PAD >= T2


def coarse_heads(own, low, high, t):
    return jnp.concatenate([own[t], (low, high)[t // 2][t % 2]], axis=1)


def coarse_forward(where, chips, mates, gain, own, low, high, even, odd, packed, kept, buf):
    me = where[0]
    for e, source in enumerate((chips, mates)):
        for d in range(4):
            columns = source[d * 8 * PAD : (d + 1) * 8 * PAD].astype(F32)
            for at in range(8):
                rows = columns[at * PAD : (at + 1) * PAD]
                to = ((at // 4 ^ e) * 4 + (at % 4 ^ d)) * PAD
                for r in range(2):
                    buf[me ^ (4 * d + 2 * r + e), to : to + PAD] = rows[:, r * 128 : (r + 1) * 128]
    pieces = [buf[n] for n in range(16)]
    units, _ = norm_parts(pieces)
    normed = []
    for n in range(16):
        lanes = slice(n * 128, (n + 1) * 128)
        kept[:, lanes] = pieces[n][:PAD].astype(BF)
        normed.append((units[n] * gain[:, lanes]).astype(BF))
    normed = jnp.concatenate(normed, axis=1)
    pack = [rounded(nn(normed, coarse_heads(own, low, high, t))) for t in range(3)]
    for t in range(3):
        packed[t] = pack[t].astype(BF)
    mixed = mix(pack[0], pack[1], pack[2], dead_keys())
    halves_out(nt(mixed, coarse_heads(own, low, high, 3)), even, odd)


def total_of(parts):
    return sum(p[...].astype(F32) for p in parts)


def coarse_finish(a, b, c, d, x, gain, out, normed):
    value = rounded(x[...].astype(F32) + total_of((a, b, c, d)))
    out[...] = value.astype(BF)
    (unit,), _ = norm_parts([value])
    normed[...] = (unit * gain[...]).astype(BF)


def lift_forward(chips, mates, own, low, high, even, odd):
    tokens = below((chips, mates))
    columns = jnp.concatenate([nn(tokens, own[...]), nn(tokens, below((low, high)))], axis=1)
    halves_out(columns, even, odd)


def sens_back(sens, to_merge, ww, merged, grad):
    value = nn(to_merge[...], sens[...])
    merged[...] = value.astype(BF)
    total = 0.0
    for s in range(4):
        total = total + nt(value[s * 72 : (s + 1) * 72], ww[:, s * C0 : (s + 1) * C0])
    grad[...] = total.astype(BF)


def member_lanes(where, e, r):
    return pl.multiple_of((2 * (where[2] ^ r) + (where[3] ^ e)) * 256, 256)


def turn_point(
    where, a, b, c, d, mid, fine, grad, gain, ww, to_nat, out, joined_grad, even, odd, wide, flat
):
    chip = where[1]
    for k, source in enumerate((a, b, c, d)):
        block = source[...].astype(F32)
        for e in range(2):
            rows = block[e * PAD : e * PAD + T2]
            for r in range(2):
                wide[chip ^ k, :, pl.ds(member_lanes(where, e, r), 256)] = rows[
                    :, r * 256 : (r + 1) * 256
                ]
    for s in range(4):
        flat[s * T2 : (s + 1) * T2] = wide[s]
    joined = rounded(mid[...].astype(F32) + flat[...])
    (unit,), scale = norm_parts([joined])
    normed = (unit * gain[...]).astype(BF)
    (back,) = norm_back([unit], scale, [grad[...].astype(F32) * gain[...]])
    joined_grad[...] = back.astype(BF)
    flat[...] = rounded(back)
    for s in range(4):
        wide[s] = flat[s * T2 : (s + 1) * T2]
    for e, target in enumerate((even, odd)):
        target[...] = jnp.zeros_like(target)
        for k in range(4):
            for r in range(2):
                target[k * PAD : k * PAD + T2, r * 256 : (r + 1) * 256] = wide[
                    chip ^ k, :, pl.ds(member_lanes(where, e, r), 256)
                ].astype(BF)
    rows = [
        fine[s * 72 : (s + 1) * 72].astype(F32) + nn(normed, ww[:, s * C0 : (s + 1) * C0])
        for s in range(4)
    ]
    out[...] = nn(to_nat[...], jnp.concatenate(rows, axis=0)).astype(BF)


def lift_back(a, b, c, d, own, low, high, even, odd):
    blocks = [v[...].astype(F32) for v in (a, b, c, d)]
    tokens = jnp.concatenate([v[:PAD] for v in blocks] + [v[PAD:] for v in blocks], axis=0)
    halves_out(nt(tokens, jnp.concatenate([own[...], below((low, high))], axis=1)), even, odd)


def coarse_out_back(a, b, c, d, value, gain, out):
    (unit,), scale = norm_parts([value[...].astype(F32)])
    cot = rounded(total_of((a, b, c, d))) * gain[...]
    out[...] = norm_back([unit], scale, [cot])[0].astype(BF)


def coarse_back(chips, mates, packed, own, low, high, even, odd):
    grad = rounded(nn(below((chips, mates)), coarse_heads(own, low, high, 3)))
    pack = [packed[t].astype(F32) for t in range(3)]
    grads = mix_back(pack[0], pack[1], pack[2], grad, dead_keys())
    halves_out(sum(nt(grads[t], coarse_heads(own, low, high, t)) for t in range(3)), even, odd)


def coarse_in_back(a, b, c, d, value, gain, grad, w, out, cot, total):
    step = pl.program_id(0)

    @pl.when(step == 0)
    def _():
        (unit,), scale = norm_parts([value[...].astype(F32)])
        back = rounded(total_of((a, b, c, d))) * gain[...]
        back = grad[...].astype(F32) + norm_back([unit], scale, [back])[0]
        for n in range(8):
            cot[n] = back[:, n * 256 : (n + 1) * 256].astype(BF)
        total[...] = jnp.zeros_like(total)

    total[...] += nt(cot[step], jnp.concatenate([w[0], w[1]], axis=1))

    @pl.when(step == 7)
    def _():
        out[...] = total[...].astype(BF)


def middle_out_back(cots, mid, gain, grad, out, buf, back):
    buf[...] = mid[...].astype(F32)
    units, scale = norm_parts([buf[s * T2 : (s + 1) * T2] for s in range(4)])
    cot = cots[:T2].astype(F32) * gain[...]
    backs = norm_back(units, scale, [cot[:, s * C1 : (s + 1) * C1] for s in range(4)])
    for s in range(4):
        back[s * T2 : (s + 1) * T2] = backs[s]
    out[...] = (grad[...].astype(F32) + back[...]).astype(BF)


def middle_back(grad, partner, x, packed, gain, w, fine, sens, mgain, mw, to_window, out):
    own = grad[...].astype(F32)
    both = jnp.concatenate([own, partner[...].astype(F32)], axis=0)
    total = 0.0
    for g in range(4):
        span = slice(g * GROUP, (g + 1) * GROUP)
        mixed = rounded(nt(both, heads_of(w, g, 3)))
        pack = [packed[t, :, span].astype(F32) for t in range(3)]
        grads = mix_back(pack[0], pack[1], pack[2], mixed)
        for t in range(3):
            total = total + nn(grads[t][:T1], heads_of(w, g, t))
    (unit,), scale = norm_parts([x[...].astype(F32)])
    into = (own + norm_back([unit], scale, [rounded(total) * gain[...]])[0]).astype(BF)
    units, scale = norm_parts([fine[s * 72 : (s + 1) * 72].astype(F32) for s in range(4)])
    cots = []
    for s in range(4):
        span = slice(s * C0, (s + 1) * C0)
        cots.append(rounded(nt(into, mw[span])) * mgain[:, span])
    backs = jnp.concatenate(norm_back(units, scale, cots), axis=0)
    out[...] = nn(to_window[...], sens[...].astype(F32) + backs).astype(BF)


def fine_back(grad, left, right, own, far, x, to_window, to_nat, gain, w, out):
    go = grad[...]
    mixed_own = rounded(nn(go, w[3]))
    mixed_far = jnp.concatenate([rounded(nn(v[...], w[3])) for v in (left, right)], axis=0)
    rows = [[], [], []]
    for at in range(0, T0, 72):
        parts = [[], [], []]
        for ch in range(0, C0, GROUP):
            span, lanes = slice(at, at + 72), slice(ch, ch + GROUP)
            pack = [
                jnp.concatenate(
                    [own[t, span, lanes].astype(F32), far[t, span, lanes].astype(F32)], axis=0
                )
                for t in range(3)
            ]
            mixed = jnp.concatenate([mixed_own[span, lanes], mixed_far[span, lanes]], axis=0)
            grads = mix_back(pack[0], pack[1], pack[2], mixed)
            for t in range(3):
                parts[t].append(grads[t][:72])
        for t in range(3):
            rows[t].append(jnp.concatenate(parts[t], axis=1))
    total = sum(nt(jnp.concatenate(rows[t], axis=0), w[t]) for t in range(3))
    (unit,), scale = norm_parts([nn(to_window[...], x[...])])
    back = go.astype(F32) + norm_back([unit], scale, [rounded(total) * gain[...]])[0]
    out[...] = nn(to_nat[...], back).astype(BF)


def local(
    latent_field,
    sensitivity,
    first_gain,
    first_proj,
    merge_gain,
    merge_weight,
    middle_gain,
    middle_proj,
    reduce_gain,
    reduce_weight,
    coarse_gain,
    coarse_proj,
    lift_gain,
    lift_weight,
    widen_gain,
    widen_weight,
):
    lat, lon = lax.axis_index("lat"), lax.axis_index("lon")
    shifted = (lon + 14) % LON
    where = jnp.stack(
        [lon, lat % 2 * 2 + shifted % 4 // 2, shifted // 4 % 2, lon % 2]
    ).astype(jnp.int32)

    def row(gain):
        return gain.reshape(1, -1)

    def flat(field):
        return field.transpose(0, 2, 1, 3).reshape(T0, C0)

    def unflat(tokens):
        return tokens.reshape(12, 12, 2, C0).transpose(0, 2, 1, 3)

    def other_shard(shard):
        at = shard.shape[0] // 2
        return send(shard[:at], NEAR), send(shard[at:], NEAR_OTHER)

    to_window = jnp.asarray(TO_WINDOW, BF)
    from_window = jnp.asarray(TO_WINDOW.T, BF)
    half = jnp.asarray(HALF_WINDOW, BF)
    to_merge = jnp.asarray(TO_MERGE, BF)
    from_merge = jnp.asarray(TO_MERGE.T, BF)
    window_to_merge = jnp.asarray(WINDOW_TO_MERGE, BF)
    merge_to_window = jnp.asarray(WINDOW_TO_MERGE.T, BF)

    mid_w = lax.all_gather(middle_proj.transpose(0, 2, 1), "lon", axis=0)
    x = flat(latent_field)
    from_left = send(x[144:], RIGHT)
    from_right = send(x[:144], LEFT)
    reduce_w = (reduce_weight, *other_shard(reduce_weight))
    coarse_w = (coarse_proj, *other_shard(coarse_proj))
    lift_w = (lift_weight, *other_shard(lift_weight))

    fine, mid_in, own, far = call(
        fine_forward,
        [((T0, C0), BF), ((T1, C1), BF), ((3, T0, C0), BF), ((3, T0, C0), BF)],
        (x, from_left, from_right, to_window, half, window_to_merge, row(first_gain), first_proj,
         row(merge_gain), merge_weight),
        vmem=24,
    )
    sens, sens_grad = call(
        sens_back,
        [((T0, C0), BF), ((T1, C1), BF)],
        (flat(sensitivity), to_merge, widen_weight),
    )
    mid_far = send(mid_in, HALF)
    mid, mid_packed, reduced = call(
        middle_forward,
        [((T1, C1), BF), ((3, 2 * T1, C1), BF), ((PAD, 4 * C1), BF)],
        (mid_in, mid_far, row(middle_gain), mid_w, row(reduce_gain)),
        scratch=[pltpu.VMEM((T1, C1), F32)],
    )
    later, _ = lax.optimization_barrier((reduce_weight, mid))
    reduce_all = lax.all_gather(later, "lon", axis=0)
    rows = 8 * PAD
    (columns_in,) = call(coarse_reduce, [((rows, 256), BF)], (*to_ring(reduced), *reduce_w))

    def halves(width):
        return [((4 * PAD, width), BF), ((4 * PAD, width), BF)]

    even, odd, coarse_packed, coarse_in = call(
        coarse_forward,
        halves(C2) + [((3, rows, 256), BF), ((PAD, C2), BF)],
        (where, *gather8(columns_in), row(coarse_gain), *coarse_w),
        1,
        scratch=[pltpu.VMEM((16, rows, 128), F32)],
    )
    coarse_out, lift_in = call(
        coarse_finish,
        [((PAD, C2), BF), ((PAD, C2), BF)],
        (*scatter8(even, odd), coarse_in, row(lift_gain)),
    )
    even, odd = call(lift_forward, halves(512), (*gather8(lift_in), *lift_w))
    predicted, joined_grad, even, odd = call(
        turn_point,
        [((T0, C0), BF), ((T1, C1), BF)] + halves(512),
        (where, *exchange8(even, odd, BACK), mid, fine, sens_grad, row(widen_gain), widen_weight,
         from_merge),
        1,
        scratch=[pltpu.VMEM((4, T2, C1), F32), pltpu.VMEM((T1, C1), F32)],
    )
    even, odd = call(lift_back, halves(C2), (*exchange8(even, odd, OUT), *lift_w))
    (coarse_grad,) = call(
        coarse_out_back, [((PAD, C2), BF)], (*scatter8(even, odd), coarse_out, row(lift_gain))
    )
    even, odd = call(coarse_back, halves(C2), (*gather8(coarse_grad), coarse_packed, *coarse_w))
    whole = pl.BlockSpec(memory_space=pltpu.VMEM)
    reduced_grad = pl.pallas_call(
        coarse_in_back,
        grid=(8,),
        out_shape=jax.ShapeDtypeStruct((PAD, 4 * C1), BF),
        in_specs=[whole] * 7 + [pl.BlockSpec((2, 4 * C1, 128), lambda n: (n, 0, 0))],
        out_specs=whole,
        scratch_shapes=[pltpu.VMEM((8, PAD, 256), BF), pltpu.VMEM((PAD, 4 * C1), F32)],
        compiler_params=pltpu.CompilerParams(vmem_limit_bytes=24 * MIB),
    )(*scatter8(even, odd), coarse_in, row(coarse_gain), coarse_grad, reduce_all)
    (mid_grad,) = call(
        middle_out_back,
        [((T1, C1), BF)],
        (send(reduced_grad, BACK[0]), mid, row(reduce_gain), joined_grad),
        scratch=[pltpu.VMEM((T1, C1), F32), pltpu.VMEM((T1, C1), F32)],
    )
    (fine_grad,) = call(
        middle_back,
        [((T0, C0), BF)],
        (mid_grad, send(mid_grad, HALF), mid_in, mid_packed, row(middle_gain), mid_w, fine,
         sens, row(merge_gain), merge_weight, merge_to_window),
        vmem=24,
    )
    grad_left = send(fine_grad[144:], RIGHT)
    grad_right = send(fine_grad[:144], LEFT)
    (result,) = call(
        fine_back,
        [((T0, C0), BF)],
        (fine_grad, grad_left, grad_right, own, far, x, to_window, from_window, row(first_gain),
         first_proj),
        vmem=24,
    )
    return unflat(predicted), unflat(result)


def solution(mesh):
    field = P("lon", None, "lat", None)
    placed = (
        field, field, P(), P(), P(), P(), P(), P(None, None, "lon"), P(), P(None, "lon"), P(),
        P(None, None, "lon"), P(), P(None, "lon"), P(), P(),
    )
    return jax.shard_map(
        local, mesh=mesh, in_specs=placed, out_specs=(field, field), check_vma=False
    )
```

```python
import jax
import jax.numpy as jnp
import numpy as np
from jax import lax
from jax.experimental import pallas as pl
from jax.experimental.pallas import tpu as pltpu
from jax.sharding import PartitionSpec as P

BF = jnp.bfloat16
F32 = jnp.float32
EPSILON = 1e-05
HD = 64
GROUP = 4 * HD
LAT, LON = 8, 16
AXES = ("lat", "lon")
T0, T1, T2 = 288, 72, 18
PAD = 24
C0, C1, C2 = 512, 1024, 2048
MIB = 1024 * 1024


def orders():
    window, merge = {}, {}
    for c in range(12):
        for lev in range(2):
            for r in range(12):
                nat = (c * 12 + r) * 2 + lev
                cw, ci, b = c // 6, c % 6 // 2, c % 2
                rw, rj, a = r // 6, r % 6 // 2, r % 2
                s = 2 * a + b
                window[nat] = (cw * 2 + rw) * 72 + s * 18 + (ci * 2 + lev) * 3 + rj
                mc, mr = c // 2, r // 2
                s1 = 2 * (mr % 2) + mc % 2
                merge[nat] = s * 72 + s1 * 18 + (mc // 2 * 2 + lev) * 3 + mr // 2
    to_window = np.zeros((T0, T0), np.float32)
    to_merge = np.zeros((T0, T0), np.float32)
    for nat in range(T0):
        to_window[window[nat], nat] = 1
        to_merge[merge[nat], nat] = 1
    half = np.zeros((144, 144), np.float32)
    for nat in range(144):
        half[window[nat], nat] = 1
    return to_window, half, to_merge


TO_WINDOW, HALF_WINDOW, TO_MERGE = orders()
WINDOW_TO_MERGE = TO_MERGE @ TO_WINDOW.T


ALONG = (0, 1, 3, 2)


def number(lat, lon):
    return lat % LAT * LON + lon % LON


def pairs_of(rule):
    return [(number(a, i), number(*rule(a, i))) for a in range(LAT) for i in range(LON)]


def member_of(lat, lon, k):
    shifted = (lon - 2) % LON
    which = (2 * (lat % 2) + shifted % 4 // 2) ^ k
    return (
        lat // 2 * 2 + which // 2,
        4 * ((shifted // 4 + ALONG[which]) % 4) + 2 * (1 - which % 2) + lon % 2,
    )


def fellow(lat, lon, k):
    which = 2 * (lat % 2) + 1 - lon // 2 % 2
    window = (lon // 4 - ALONG[which]) % 4
    which ^= k
    return (
        lat // 2 * 2 + which // 2,
        4 * ((window + ALONG[which]) % 4) + 2 * (1 - which % 2) + lon % 2,
    )


def table(rule):
    return np.array(
        [[[rule(a, i, k)[1] for k in range(4)] for i in range(LON)] for a in range(2)], np.int32
    )


OUT = [pairs_of(lambda a, i, k=k: member_of(a, i, k)) for k in range(4)]
BACK = [[(target, source) for source, target in pairs] for pairs in OUT]
RING = [pairs_of(lambda a, i, k=k: fellow(a, i, k)) for k in range(4)]
CORE = pairs_of(lambda a, i: (a, i ^ 1))
NEAR = pairs_of(lambda a, i: (a ^ 1, i ^ 2))
RIGHT = pairs_of(lambda a, i: (a, i + 1))
LEFT = pairs_of(lambda a, i: (a, i - 1))
HALF = pairs_of(lambda a, i: (a, i + 1 if i % 2 else i - 1))


def send(value, pairs):
    return lax.ppermute(value, AXES, pairs)


def to_ring(block):
    chips = jnp.concatenate([send(block, OUT[k]) for k in range(4)])
    return chips, send(chips, CORE)


def gather8(block):
    chips = jnp.concatenate([block] + [send(block, RING[k]) for k in (1, 2, 3)])
    return chips, send(chips, CORE)


def scatter8(even, odd):
    both = (even.astype(F32) + send(odd, CORE).astype(F32)).astype(BF)
    parts = [both[k * PAD : (k + 1) * PAD] for k in range(4)]
    return [parts[0]] + [send(parts[k], RING[k]) for k in (1, 2, 3)]


def exchange8(even, odd, ways):
    other = send(odd, CORE)
    return [
        send(jnp.concatenate([even[k * PAD : (k + 1) * PAD], other[k * PAD : (k + 1) * PAD]]), ways[k])
        for k in range(4)
    ]


def nn(a, b):
    return lax.dot_general(
        a.astype(BF), b.astype(BF), (((1,), (0,)), ((), ())), preferred_element_type=F32
    )


def nt(a, b):
    return lax.dot_general(
        a.astype(BF), b.astype(BF), (((1,), (1,)), ((), ())), preferred_element_type=F32
    )


def tn(a, b):
    return lax.dot_general(
        a.astype(BF), b.astype(BF), (((0,), (0,)), ((), ())), preferred_element_type=F32
    )


def rounded(value):
    return value.astype(BF).astype(F32)


def norm_parts(pieces):
    width = sum(v.shape[1] for v in pieces)
    mean = sum(jnp.sum(v, axis=1, keepdims=True) for v in pieces) / width
    centred = [v - mean for v in pieces]
    spread = sum(jnp.sum(v * v, axis=1, keepdims=True) for v in centred) / width
    scale = lax.rsqrt(spread + EPSILON)
    return [v * scale for v in centred], scale


def norm_back(unit, scale, cot):
    width = sum(v.shape[1] for v in unit)
    first = sum(jnp.sum(v, axis=1, keepdims=True) for v in cot) / width
    second = sum(jnp.sum(v * u, axis=1, keepdims=True) for v, u in zip(cot, unit)) / width
    return [scale * (v - first - u * second) for v, u in zip(cot, unit)]


def head_masks():
    lane = lax.broadcasted_iota(jnp.int32, (1, GROUP), 1) // HD
    return [(lane == h).astype(F32) for h in range(4)]


def by_head(value):
    return jnp.concatenate([value * m for m in head_masks()], axis=0)


def own_heads(value, rows):
    return sum(value[h * rows : (h + 1) * rows] * m for h, m in enumerate(head_masks()))


def weights_of(q, k, dead):
    scores = nt(by_head(q), k) * HD ** (-0.5)
    if dead is not None:
        scores = jnp.where(dead, -1e30, scores)
    raised = jnp.exp(scores - jnp.max(scores, axis=1, keepdims=True))
    return raised / jnp.sum(raised, axis=1, keepdims=True)


def mix(q, k, v, dead=None):
    return rounded(own_heads(nn(weights_of(q, k, dead), v), q.shape[0]))


def mix_back(q, k, v, grad, dead=None):
    rows = q.shape[0]
    weights = weights_of(q, k, dead)
    grads = by_head(grad)
    from_weights = nt(grads, v)
    inner = jnp.sum(weights * from_weights, axis=1, keepdims=True)
    from_scores = weights * (from_weights - inner) * HD ** (-0.5)
    return (
        rounded(own_heads(nn(from_scores, k), rows)),
        rounded(tn(from_scores, by_head(q))),
        rounded(tn(weights, grads)),
    )


class Scalars:
    def __init__(self, array):
        self.array = array


class Far:
    def __init__(self, array, parts=1):
        self.array, self.parts = array, parts


class Quarters(Far):
    pass


class Joined:
    def __init__(self, source, held, sems):
        self.held, self.waiting = held, set(range(4))
        self.copies = [
            pltpu.make_async_copy(source.at[:, t], held.at[t], sems.at[t]) for t in range(4)
        ]
        for copy in self.copies:
            copy.start()

    def __getitem__(self, t):
        if t in self.waiting:
            self.copies[t].wait()
            self.waiting.remove(t)
        value = self.held[t]
        return value.reshape(-1, value.shape[-1])


class Fetched:
    def __init__(self, source, held, sems, parts):
        self.held, self.size = held, source.shape[0] // parts
        self.copies = [
            pltpu.make_async_copy(
                source.at[pl.ds(n * self.size, self.size)],
                held.at[pl.ds(n * self.size, self.size)],
                sems.at[n],
            )
            for n in range(parts)
        ]
        for copy in self.copies:
            copy.start()
        self.waiting = set(range(parts))

    def __getitem__(self, at):
        lead = at[0] if isinstance(at, tuple) else at
        if isinstance(lead, int):
            wanted = {lead // self.size}
        elif isinstance(lead, slice):
            first, last, _ = lead.indices(self.held.shape[0])
            wanted = set(range(first // self.size, (last - 1) // self.size + 1))
        else:
            wanted = set(self.waiting)
        for n in sorted(wanted & self.waiting):
            self.copies[n].wait()
        self.waiting -= wanted
        return self.held[at]


class Kept:
    def __init__(self, target, held, sem):
        self.held, self.copy, self.open = held, pltpu.make_async_copy(held, target, sem), True

    def __setitem__(self, at, value):
        self.held[at] = value

    def flush(self):
        self.open = False
        self.copy.start()


def call(body, outs, args, scratch=(), vmem=32):
    specs, arrays, extra = [], [], []
    for arg in args:
        if isinstance(arg, Scalars):
            specs.append(pl.BlockSpec(memory_space=pltpu.SMEM))
            arrays.append(arg.array)
        elif isinstance(arg, Far):
            specs.append(pl.BlockSpec(memory_space=pltpu.HBM))
            arrays.append(pltpu.with_memory_space_constraint(arg.array, pltpu.HBM))
            extra.append(pltpu.VMEM(arg.array.shape, arg.array.dtype))
            extra.append(pltpu.SemaphoreType.DMA((arg.parts,)))
        else:
            specs.append(pl.BlockSpec(memory_space=pltpu.VMEM))
            arrays.append(arg)
    for shape, own in outs:
        if own:
            extra.append(pltpu.VMEM(shape, BF))
            extra.append(pltpu.SemaphoreType.DMA)

    def kernel(*refs):
        ins, rest = list(refs[: len(specs)]), refs[len(specs) :]
        targets, rest = rest[: len(outs)], rest[len(outs) :]
        buffers, rest = rest[: len(scratch)], list(rest[len(scratch) :])
        given = []
        for arg in args:
            ref = ins.pop(0)
            if isinstance(arg, Quarters):
                given.append(Joined(ref, rest.pop(0), rest.pop(0)))
            elif isinstance(arg, Far):
                given.append(Fetched(ref, rest.pop(0), rest.pop(0), arg.parts))
            else:
                given.append(ref)
        kept = []
        for (_, own), ref in zip(outs, targets):
            kept.append(Kept(ref, rest.pop(0), rest.pop(0)) if own else ref)
        body(*given, *kept, *buffers)
        for held in kept:
            if isinstance(held, Kept):
                if held.open:
                    held.flush()
                held.copy.wait()
        for held in given:
            if isinstance(held, (Fetched, Joined)):
                for n in sorted(held.waiting):
                    held.copies[n].wait()

    return pl.pallas_call(
        kernel,
        out_shape=[
            pltpu.HBM(shape, BF) if own else jax.ShapeDtypeStruct(shape, BF) for shape, own in outs
        ],
        in_specs=specs,
        out_specs=[
            pl.BlockSpec(memory_space=pltpu.HBM if own else pltpu.VMEM) for _, own in outs
        ],
        scratch_shapes=list(scratch) + extra,
        compiler_params=pltpu.CompilerParams(vmem_limit_bytes=vmem * MIB),
        cost_estimate=pl.CostEstimate(flops=1, bytes_accessed=1, transcendentals=0),
    )(*arrays)


def fine_forward(x, left, right, to_window, half, to_merge, gain, w, mgain, mw, fine, mid, own, far):
    xo = nn(to_window[...], x[...])
    xh = jnp.concatenate([nn(half[...], left[...]), nn(half[...], right[...])], axis=0)
    packs = []
    for value, kept in ((xo, own), (xh, far)):
        (unit,), _ = norm_parts([value])
        normed = (unit * gain[...]).astype(BF)
        pack = [rounded(nn(normed, w[t])) for t in range(3)]
        for t in range(3):
            kept[t] = pack[t].astype(BF)
        kept.flush()
        packs.append(pack)
    rows = []
    for at in range(0, T0, 72):
        parts = []
        for ch in range(0, C0, GROUP):
            q = packs[0][0][at : at + 72, ch : ch + GROUP]
            k, v = [
                jnp.concatenate([pk[t][at : at + 72, ch : ch + GROUP] for pk in packs], axis=0)
                for t in (1, 2)
            ]
            parts.append(mix(q, k, v))
        rows.append(jnp.concatenate(parts, axis=1))
    mixed = jnp.concatenate(rows, axis=0)
    out = rounded(xo + nt(mixed, w[3]))
    merged = nn(to_merge[...], out)
    fine[...] = merged.astype(BF)
    units, _ = norm_parts([merged[s * 72 : (s + 1) * 72] for s in range(4)])
    total = 0.0
    for s in range(4):
        span = slice(s * C0, (s + 1) * C0)
        total = total + nn(units[s] * mgain[:, span], mw[span])
    mid[...] = total.astype(BF)


def heads_of(w, g, t):
    return jnp.concatenate([w[4 * g + h, t] for h in range(4)], axis=0)


def middle_forward(x, partner, gain, w, rgain, out, packed, reduced, buf):
    own = x[...].astype(F32)
    both = jnp.concatenate([own, partner[...].astype(F32)], axis=0)
    (unit,), _ = norm_parts([both])
    normed = (unit * gain[...]).astype(BF)
    total = own
    for g in range(4):
        span = slice(g * GROUP, (g + 1) * GROUP)
        pack = [rounded(nt(normed, heads_of(w, g, t))) for t in range(3)]
        for t in range(3):
            packed[t, :, span] = pack[t].astype(BF)
        total = total + nn(mix(pack[0][:T1], pack[1], pack[2]), heads_of(w, g, 3))
    out[...] = total.astype(BF)
    buf[...] = rounded(total)
    units, _ = norm_parts([buf[s * T2 : (s + 1) * T2] for s in range(4)])
    reduced[...] = jnp.zeros_like(reduced)
    for s in range(4):
        span = slice(s * C1, (s + 1) * C1)
        reduced[:T2, span] = (units[s] * rgain[:, span]).astype(BF)


def beside(parts):
    return jnp.concatenate([part[...] for part in parts], axis=1)


def below(parts):
    return jnp.concatenate([part[...] for part in parts], axis=0)


def halves_out(value, even, odd):
    even[...] = value[: 4 * PAD].astype(BF)
    odd[...] = value[4 * PAD :].astype(BF)


def coarse_reduce(chips, mates, own, other, out):
    tokens = below((chips, mates))
    out[:, :128] = nn(tokens, own[...]).astype(BF)
    out[:, 128:] = nn(tokens, other[...]).astype(BF)


def dead_keys():
    return lax.broadcasted_iota(jnp.int32, (1, 8 * PAD), 1) % PAD >= T2


def coarse_heads(own, others, t):
    return jnp.concatenate([own[t], others[t]], axis=1)


def coarse_forward(where, chips, mates, gain, own, others, even, odd, packed, kept, buf):
    for e, source in enumerate((chips, mates)):
        for d in range(4):
            columns = source[d * 8 * PAD : (d + 1) * 8 * PAD].astype(F32)
            for at in range(8):
                rows = columns[at * PAD : (at + 1) * PAD]
                to = ((at // 4 ^ e) * 4 + (at % 4 ^ d)) * PAD
                for r in range(2):
                    buf[where[d] ^ (2 * r + e), to : to + PAD] = rows[:, r * 128 : (r + 1) * 128]
    pieces = [buf[n] for n in range(16)]
    units, _ = norm_parts(pieces)
    normed = []
    for n in range(16):
        lanes = slice(n * 128, (n + 1) * 128)
        kept[:, lanes] = pieces[n][:PAD].astype(BF)
        normed.append((units[n] * gain[:, lanes]).astype(BF))
    normed = jnp.concatenate(normed, axis=1)
    pack = [rounded(nn(normed, coarse_heads(own, others, t))) for t in range(3)]
    for t in range(3):
        packed[t] = pack[t].astype(BF)
    mixed = mix(pack[0], pack[1], pack[2], dead_keys())
    halves_out(nt(mixed, coarse_heads(own, others, 3)), even, odd)


def total_of(parts):
    return sum(p[...].astype(F32) for p in parts)


def coarse_finish(a, b, c, d, x, gain, out, normed):
    value = rounded(x[...].astype(F32) + total_of((a, b, c, d)))
    out[...] = value.astype(BF)
    (unit,), _ = norm_parts([value])
    normed[...] = (unit * gain[...]).astype(BF)


def lift_forward(chips, mates, own, other, even, odd):
    tokens = below((chips, mates))
    columns = nn(tokens, beside((own, other)))
    halves_out(columns, even, odd)


def sens_back(sens, to_merge, ww, merged, grad):
    value = nn(to_merge[...], sens[...])
    merged[...] = value.astype(BF)
    total = 0.0
    for s in range(4):
        total = total + nt(value[s * 72 : (s + 1) * 72], ww[:, s * C0 : (s + 1) * C0])
    grad[...] = total.astype(BF)


def member_lanes(where, k, e, r):
    return pl.multiple_of((where[4 + k] % 4 ^ (2 * r + e)) * 256, 256)


def turn_point(
    where, a, b, c, d, mid, fine, grad, gain, ww, to_nat, out, joined_grad, even, odd, wide, flat
):
    for k, source in enumerate((a, b, c, d)):
        block = source[...].astype(F32)
        for e in range(2):
            rows = block[e * PAD : e * PAD + T2]
            for r in range(2):
                wide[where[4 + k] // 4, :, pl.ds(member_lanes(where, k, e, r), 256)] = rows[
                    :, r * 256 : (r + 1) * 256
                ]
    for s in range(4):
        flat[s * T2 : (s + 1) * T2] = wide[s]
    joined = rounded(mid[...].astype(F32) + flat[...])
    (unit,), scale = norm_parts([joined])
    normed = (unit * gain[...]).astype(BF)
    (back,) = norm_back([unit], scale, [grad[...].astype(F32) * gain[...]])
    joined_grad[...] = back.astype(BF)
    flat[...] = rounded(back)
    for s in range(4):
        wide[s] = flat[s * T2 : (s + 1) * T2]
    for e, target in enumerate((even, odd)):
        target[...] = jnp.zeros_like(target)
        for k in range(4):
            for r in range(2):
                target[k * PAD : k * PAD + T2, r * 256 : (r + 1) * 256] = wide[
                    where[4 + k] // 4, :, pl.ds(member_lanes(where, k, e, r), 256)
                ].astype(BF)
    rows = [
        fine[s * 72 : (s + 1) * 72].astype(F32) + nn(normed, ww[:, s * C0 : (s + 1) * C0])
        for s in range(4)
    ]
    out[...] = nn(to_nat[...], jnp.concatenate(rows, axis=0)).astype(BF)


def lift_back(a, b, c, d, own, other, even, odd):
    blocks = [v[...].astype(F32) for v in (a, b, c, d)]
    tokens = jnp.concatenate([v[:PAD] for v in blocks] + [v[PAD:] for v in blocks], axis=0)
    halves_out(nt(tokens, beside((own, other))), even, odd)


def coarse_out_back(a, b, c, d, value, gain, out):
    (unit,), scale = norm_parts([value[...].astype(F32)])
    cot = rounded(total_of((a, b, c, d))) * gain[...]
    out[...] = norm_back([unit], scale, [cot])[0].astype(BF)


def coarse_back(chips, mates, packed, own, others, even, odd):
    grad = rounded(nn(below((chips, mates)), coarse_heads(own, others, 3)))
    pack = [packed[t].astype(F32) for t in range(3)]
    grads = mix_back(pack[0], pack[1], pack[2], grad, dead_keys())
    halves_out(sum(nt(grads[t], coarse_heads(own, others, t)) for t in range(3)), even, odd)


def coarse_in_back(a, b, c, d, value, gain, grad, w, out):
    (unit,), scale = norm_parts([value[...].astype(F32)])
    cot = rounded(total_of((a, b, c, d))) * gain[...]
    cot = (grad[...].astype(F32) + norm_back([unit], scale, [cot])[0]).astype(BF)
    total = 0.0
    for n in range(8):
        shards = jnp.concatenate([w[2 * n], w[2 * n + 1]], axis=1)
        total = total + nt(cot[:, n * 256 : (n + 1) * 256], shards)
    out[...] = total.astype(BF)


def middle_out_back(cots, mid, gain, grad, out, buf, back):
    buf[...] = mid[...].astype(F32)
    units, scale = norm_parts([buf[s * T2 : (s + 1) * T2] for s in range(4)])
    cot = cots[:T2].astype(F32) * gain[...]
    backs = norm_back(units, scale, [cot[:, s * C1 : (s + 1) * C1] for s in range(4)])
    for s in range(4):
        back[s * T2 : (s + 1) * T2] = backs[s]
    out[...] = (grad[...].astype(F32) + back[...]).astype(BF)


def middle_back(grad, partner, x, packed, gain, w, fine, sens, mgain, mw, to_window, out):
    own = grad[...].astype(F32)
    both = jnp.concatenate([own, partner[...].astype(F32)], axis=0)
    total = 0.0
    for g in range(4):
        span = slice(g * GROUP, (g + 1) * GROUP)
        mixed = rounded(nt(both, heads_of(w, g, 3)))
        pack = [packed[t, :, span].astype(F32) for t in range(3)]
        grads = mix_back(pack[0], pack[1], pack[2], mixed)
        for t in range(3):
            total = total + nn(grads[t][:T1], heads_of(w, g, t))
    (unit,), scale = norm_parts([x[...].astype(F32)])
    into = (own + norm_back([unit], scale, [rounded(total) * gain[...]])[0]).astype(BF)
    units, scale = norm_parts([fine[s * 72 : (s + 1) * 72].astype(F32) for s in range(4)])
    cots = []
    for s in range(4):
        span = slice(s * C0, (s + 1) * C0)
        cots.append(rounded(nt(into, mw[span])) * mgain[:, span])
    backs = jnp.concatenate(norm_back(units, scale, cots), axis=0)
    out[...] = nn(to_window[...], sens[...].astype(F32) + backs).astype(BF)


def fine_back(grad, left, right, own, far, x, to_window, to_nat, gain, w, out):
    go = grad[...]
    mixed_own = rounded(nn(go, w[3]))
    mixed_far = jnp.concatenate([rounded(nn(v[...], w[3])) for v in (left, right)], axis=0)
    rows = [[], [], []]
    for at in range(0, T0, 72):
        parts = [[], [], []]
        for ch in range(0, C0, GROUP):
            span, lanes = slice(at, at + 72), slice(ch, ch + GROUP)
            pack = [
                jnp.concatenate(
                    [own[t, span, lanes].astype(F32), far[t, span, lanes].astype(F32)], axis=0
                )
                for t in range(3)
            ]
            mixed = jnp.concatenate([mixed_own[span, lanes], mixed_far[span, lanes]], axis=0)
            grads = mix_back(pack[0], pack[1], pack[2], mixed)
            for t in range(3):
                parts[t].append(grads[t][:72])
        for t in range(3):
            rows[t].append(jnp.concatenate(parts[t], axis=1))
    total = sum(nt(jnp.concatenate(rows[t], axis=0), w[t]) for t in range(3))
    (unit,), scale = norm_parts([nn(to_window[...], x[...])])
    back = go.astype(F32) + norm_back([unit], scale, [rounded(total) * gain[...]])[0]
    out[...] = nn(to_nat[...], back).astype(BF)


def local(
    latent_field,
    sensitivity,
    first_gain,
    first_proj,
    merge_gain,
    merge_weight,
    middle_gain,
    middle_proj,
    reduce_gain,
    reduce_weight,
    coarse_gain,
    coarse_proj,
    lift_gain,
    lift_weight,
    widen_gain,
    widen_weight,
):
    lat, lon = lax.axis_index("lat"), lax.axis_index("lon")
    places = [jnp.asarray(table(rule))[lat % 2, lon] for rule in (fellow, member_of)]
    where = Scalars(jnp.concatenate(places))

    def row(gain):
        return Far(gain.reshape(1, -1))

    def flat(field):
        return field.transpose(0, 2, 1, 3).reshape(T0, C0)

    def unflat(tokens):
        return tokens.reshape(12, 12, 2, C0).transpose(0, 2, 1, 3)

    def both_ways(shard):
        at = shard.shape[0] // 2
        return send(shard[:at], NEAR), send(shard[at:], NEAR_OTHER)

    def after(value, *others):
        return lax.optimization_barrier((value, *others))

    def order(matrix):
        return Far(jnp.asarray(matrix, BF))

    mid_w = lax.all_gather(middle_proj.transpose(0, 2, 1), "lon", axis=0)
    x = flat(latent_field)
    from_left = send(x[144:], RIGHT)
    from_right = send(x[:144], LEFT)
    def quarter(shard, axis):
        size = shard.shape[axis] // 4
        return lax.dynamic_slice_in_dim(shard, lat // 2 * size, size, axis)

    def over_x(part):
        return lax.all_gather(
            part, "lat", axis_index_groups=[[p, p + 2, p + 4, p + 6] for p in range(2)], axis=0
        )

    reduce_other = send(reduce_weight, NEAR)
    coarse_part = send(quarter(coarse_proj, 1), NEAR)
    lift_part = send(quarter(lift_weight, 0), NEAR)

    def after(value, *others):
        return lax.optimization_barrier((value, *others))

    def order(matrix):
        return Far(jnp.asarray(matrix, BF))

    mid_w = lax.all_gather(middle_proj.transpose(0, 2, 1), "lon", axis=0)
    x = flat(latent_field)
    from_left = send(x[144:], RIGHT)
    from_right = send(x[:144], LEFT)
    place = (lat // 2).astype(jnp.int32).reshape(1)

    def quarter(shard, axis):
        size = shard.shape[axis] // 4
        return lax.dynamic_slice_in_dim(shard, lat // 2 * size, size, axis)

    reduce_part, packed_part, back_part, lift_part = [
        send(v, NEAR)
        for v in (
            quarter(reduce_weight, 0),
            quarter(coarse_proj[:3], 1),
            quarter(coarse_proj[3], 0),
            quarter(lift_weight, 0),
        )
    ]

    def sides(part):
        return [send(part, SIDE[k]) for k in (1, 2, 3)]

    def after(value, *others):
        return lax.optimization_barrier((value, *others))

    def order(matrix):
        return Far(jnp.asarray(matrix, BF))

    x, reduce_other = after(x, reduce_other)
    reduce_w = (Far(reduce_weight), Far(reduce_other))
    fine, mid_in, own, far = call(
        fine_forward,
        [((T0, C0), False), ((T1, C1), False), ((3, T0, C0), True), ((3, T0, C0), True)],
        (x, from_left, from_right, order(TO_WINDOW), order(HALF_WINDOW), order(WINDOW_TO_MERGE),
         row(first_gain), Far(first_proj, 4), row(merge_gain), Far(merge_weight, 4)),
    )
    sens, sens_grad = call(
        sens_back,
        [((T0, C0), False), ((T1, C1), False)],
        (flat(sensitivity), order(TO_MERGE), Far(widen_weight)),
    )
    mid_in, coarse_part, lift_part = after(mid_in, coarse_part, lift_part)
    mid_far = send(mid_in, HALF)
    coarse_w = (Far(coarse_proj, 4), Quarters(over_x(coarse_part), 4))
    lift_w = (Far(lift_weight), Far(over_x(lift_part).reshape(C2, 256)))
    mid, mid_packed, reduced = call(
        middle_forward,
        [((T1, C1), False), ((3, 2 * T1, C1), True), ((PAD, 4 * C1), False)],
        (mid_in, mid_far, row(middle_gain), Far(mid_w, 4), row(reduce_gain)),
        scratch=[pltpu.VMEM((T1, C1), F32)],
    )
    later, _ = after(reduce_weight, mid)
    reduce_all = lax.all_gather(later, "lon", axis=0)
    rows = 8 * PAD
    (columns_in,) = call(coarse_reduce, [((rows, 256), False)], (*to_ring(reduced), *reduce_w))


    def halves(width):
        return [((4 * PAD, width), False), ((4 * PAD, width), False)]

    even, odd, coarse_packed, coarse_in = call(
        coarse_forward,
        halves(C2) + [((3, rows, 256), False), ((PAD, C2), False)],
        (where, *gather8(columns_in), row(coarse_gain), *coarse_w),
        scratch=[pltpu.VMEM((16, rows, 128), F32)],
    )
    coarse_out, lift_in = call(
        coarse_finish,
        [((PAD, C2), False), ((PAD, C2), False)],
        (*scatter8(even, odd), coarse_in, row(lift_gain)),
    )
    even, odd = call(lift_forward, halves(512), (*gather8(lift_in), *lift_w))
    predicted, joined_grad, even, odd = call(
        turn_point,
        [((T0, C0), False), ((T1, C1), False)] + halves(512),
        (where, *exchange8(even, odd, BACK), mid, Far(fine), Far(sens_grad), row(widen_gain),
         Far(widen_weight), order(TO_MERGE.T)),
        scratch=[pltpu.VMEM((4, T2, C1), F32), pltpu.VMEM((T1, C1), F32)],
    )
    even, odd = call(lift_back, halves(C2), (*exchange8(even, odd, OUT), *lift_w))
    (coarse_grad,) = call(
        coarse_out_back, [((PAD, C2), False)], (*scatter8(even, odd), coarse_out, row(lift_gain))
    )
    even, odd = call(
        coarse_back, halves(C2), (*gather8(coarse_grad), Far(coarse_packed), *coarse_w)
    )
    (reduced_grad,) = call(
        coarse_in_back,
        [((PAD, 4 * C1), False)],
        (*scatter8(even, odd), coarse_in, row(coarse_gain), coarse_grad, Far(reduce_all, 8)),
    )
    (mid_grad,) = call(
        middle_out_back,
        [((T1, C1), False)],
        (send(reduced_grad, BACK[0]), mid, row(reduce_gain), joined_grad),
        scratch=[pltpu.VMEM((T1, C1), F32), pltpu.VMEM((T1, C1), F32)],
    )
    (fine_grad,) = call(
        middle_back,
        [((T0, C0), False)],
        (mid_grad, send(mid_grad, HALF), mid_in, Far(mid_packed), row(middle_gain), Far(mid_w, 4),
         Far(fine), Far(sens), row(merge_gain), Far(merge_weight, 4), order(WINDOW_TO_MERGE.T)),
    )
    grad_left = send(fine_grad[144:], RIGHT)
    grad_right = send(fine_grad[:144], LEFT)
    (result,) = call(
        fine_back,
        [((T0, C0), False)],
        (fine_grad, grad_left, grad_right, Far(own), Far(far), Far(x), order(TO_WINDOW),
         order(TO_WINDOW.T), row(first_gain), Far(first_proj, 4)),
    )
    return unflat(predicted), unflat(result)


def solution(mesh):
    field = P("lon", None, "lat", None)
    placed = (
        field, field, P(), P(), P(), P(), P(), P(None, None, "lon"), P(), P(None, "lon"), P(),
        P(None, None, "lon"), P(), P(None, "lon"), P(), P(),
    )
    return jax.shard_map(
        local, mesh=mesh, in_specs=placed, out_specs=(field, field), check_vma=False
    )
```

```python
import jax
import jax.numpy as jnp
import numpy as np
from jax import lax
from jax.experimental import pallas as pl
from jax.experimental.pallas import tpu as pltpu
from jax.sharding import PartitionSpec as P

BF = jnp.bfloat16
F32 = jnp.float32
EPSILON = 1e-05
HD = 64
GROUP = 4 * HD
LAT, LON = 8, 16
AXES = ("lat", "lon")
T0, T1, T2 = 288, 72, 18
PAD = 24
C0, C1, C2 = 512, 1024, 2048
MIB = 1024 * 1024


def orders():
    window, merge = {}, {}
    for c in range(12):
        for lev in range(2):
            for r in range(12):
                nat = (c * 12 + r) * 2 + lev
                cw, ci, b = c // 6, c % 6 // 2, c % 2
                rw, rj, a = r // 6, r % 6 // 2, r % 2
                s = 2 * a + b
                window[nat] = (cw * 2 + rw) * 72 + s * 18 + (ci * 2 + lev) * 3 + rj
                mc, mr = c // 2, r // 2
                s1 = 2 * (mr % 2) + mc % 2
                merge[nat] = s * 72 + s1 * 18 + (mc // 2 * 2 + lev) * 3 + mr // 2
    to_window = np.zeros((T0, T0), np.float32)
    to_merge = np.zeros((T0, T0), np.float32)
    for nat in range(T0):
        to_window[window[nat], nat] = 1
        to_merge[merge[nat], nat] = 1
    half = np.zeros((144, 144), np.float32)
    for nat in range(144):
        half[window[nat], nat] = 1
    return to_window, half, to_merge


TO_WINDOW, HALF_WINDOW, TO_MERGE = orders()
WINDOW_TO_MERGE = TO_MERGE @ TO_WINDOW.T


ALONG = (0, 1, 3, 2)


def number(lat, lon):
    return lat % LAT * LON + lon % LON


def pairs_of(rule):
    return [(number(a, i), number(*rule(a, i))) for a in range(LAT) for i in range(LON)]


def member_of(lat, lon, k):
    shifted = (lon - 2) % LON
    which = (2 * (lat % 2) + shifted % 4 // 2) ^ k
    return (
        lat // 2 * 2 + which // 2,
        4 * ((shifted // 4 + ALONG[which]) % 4) + 2 * (1 - which % 2) + lon % 2,
    )


def fellow(lat, lon, k):
    which = 2 * (lat % 2) + 1 - lon // 2 % 2
    window = (lon // 4 - ALONG[which]) % 4
    which ^= k
    return (
        lat // 2 * 2 + which // 2,
        4 * ((window + ALONG[which]) % 4) + 2 * (1 - which % 2) + lon % 2,
    )


def table(rule):
    return np.array(
        [[[rule(a, i, k)[1] for k in range(4)] for i in range(LON)] for a in range(2)], np.int32
    )


OUT = [pairs_of(lambda a, i, k=k: member_of(a, i, k)) for k in range(4)]
BACK = [[(target, source) for source, target in pairs] for pairs in OUT]
RING = [pairs_of(lambda a, i, k=k: fellow(a, i, k)) for k in range(4)]
CORE = pairs_of(lambda a, i: (a, i ^ 1))
NEAR = pairs_of(lambda a, i: (a ^ 1, i ^ 2))
RIGHT = pairs_of(lambda a, i: (a, i + 1))
LEFT = pairs_of(lambda a, i: (a, i - 1))
HALF = pairs_of(lambda a, i: (a, i + 1 if i % 2 else i - 1))


def send(value, pairs):
    return lax.ppermute(value, AXES, pairs)


def after(value, *others):
    return lax.optimization_barrier((value, *others))


def across(parts, meanwhile):
    chips, *meanwhile = after(jnp.concatenate(parts), *meanwhile)
    return (chips, send(chips, CORE)), meanwhile


def to_ring(block, *meanwhile):
    return across([send(block, OUT[k]) for k in range(4)], meanwhile)


def gather8(block, *meanwhile):
    return across([block] + [send(block, RING[k]) for k in (1, 2, 3)], meanwhile)


def scatter8(even, odd):
    both = (even.astype(F32) + send(odd, CORE).astype(F32)).astype(BF)
    parts = [both[k * PAD : (k + 1) * PAD] for k in range(4)]
    return [parts[0]] + [send(parts[k], RING[k]) for k in (1, 2, 3)]


def exchange8(even, odd, ways):
    other = send(odd, CORE)
    return [
        send(jnp.concatenate([even[k * PAD : (k + 1) * PAD], other[k * PAD : (k + 1) * PAD]]), ways[k])
        for k in range(4)
    ]


def nn(a, b):
    return lax.dot_general(
        a.astype(BF), b.astype(BF), (((1,), (0,)), ((), ())), preferred_element_type=F32
    )


def nt(a, b):
    return lax.dot_general(
        a.astype(BF), b.astype(BF), (((1,), (1,)), ((), ())), preferred_element_type=F32
    )


def tn(a, b):
    return lax.dot_general(
        a.astype(BF), b.astype(BF), (((0,), (0,)), ((), ())), preferred_element_type=F32
    )


def rounded(value):
    return value.astype(BF).astype(F32)


def norm_parts(pieces):
    width = sum(v.shape[1] for v in pieces)
    mean = sum(jnp.sum(v, axis=1, keepdims=True) for v in pieces) / width
    centred = [v - mean for v in pieces]
    spread = sum(jnp.sum(v * v, axis=1, keepdims=True) for v in centred) / width
    scale = lax.rsqrt(spread + EPSILON)
    return [v * scale for v in centred], scale


def norm_back(unit, scale, cot):
    width = sum(v.shape[1] for v in unit)
    first = sum(jnp.sum(v, axis=1, keepdims=True) for v in cot) / width
    second = sum(jnp.sum(v * u, axis=1, keepdims=True) for v, u in zip(cot, unit)) / width
    return [scale * (v - first - u * second) for v, u in zip(cot, unit)]


def head_masks():
    lane = lax.broadcasted_iota(jnp.int32, (1, GROUP), 1) // HD
    return [(lane == h).astype(F32) for h in range(4)]


def by_head(value):
    return jnp.concatenate([value * m for m in head_masks()], axis=0)


def own_heads(value, rows):
    return sum(value[h * rows : (h + 1) * rows] * m for h, m in enumerate(head_masks()))


def weights_of(q, k, dead=None):
    scores = nt(k, by_head(q)) * HD ** (-0.5)
    if dead is not None:
        scores = jnp.where(dead, -1e30, scores)
    raised = jnp.exp(scores - jnp.max(scores, axis=0, keepdims=True))
    return raised / jnp.sum(raised, axis=0, keepdims=True)


def mix(q, k, v, dead=None):
    return rounded(own_heads(tn(weights_of(q, k, dead), v), q.shape[0]))


def mix_back(q, k, v, grad, weights):
    grads = by_head(grad)
    from_weights = nt(v, grads)
    soft = weights.astype(F32)
    inner = jnp.sum(soft * from_weights, axis=0, keepdims=True)
    from_scores = soft * (from_weights - inner) * HD ** (-0.5)
    return (
        rounded(own_heads(tn(from_scores, k), q.shape[0])),
        rounded(nn(from_scores, by_head(q))),
        rounded(nn(weights, grads)),
    )


class Scalars:
    def __init__(self, array):
        self.array = array


class Far:
    def __init__(self, array, parts=1):
        self.array, self.parts = array, parts

    def with_array(self, array):
        return Far(array, self.parts)


class Quarters:
    def __init__(self, array, first, count):
        self.array, self.first, self.count = array, first, count

    def with_array(self, array):
        return Quarters(array, self.first, self.count)


class JoinedHere:
    def __init__(self, array):
        self.array = array


class Rows:
    def __init__(self, ref):
        self.ref = ref

    def __getitem__(self, t):
        value = self.ref[t]
        return value.reshape(-1, value.shape[-1])


class Fetched:
    def __init__(self, source, held, sems, parts):
        self.held, self.size = held, source.shape[0] // parts
        self.copies = [
            pltpu.make_async_copy(
                source.at[pl.ds(n * self.size, self.size)],
                held.at[pl.ds(n * self.size, self.size)],
                sems.at[n],
            )
            for n in range(parts)
        ]
        for copy in self.copies:
            copy.start()
        self.waiting = set(range(parts))

    def __getitem__(self, at):
        lead = at[0] if isinstance(at, tuple) else at
        if isinstance(lead, int):
            wanted = {lead // self.size}
        elif isinstance(lead, slice):
            first, last, _ = lead.indices(self.held.shape[0])
            wanted = set(range(first // self.size, (last - 1) // self.size + 1))
        else:
            wanted = set(self.waiting)
        for n in sorted(wanted & self.waiting):
            self.copies[n].wait()
        self.waiting -= wanted
        return self.held[at]


class Kept:
    def __init__(self, target, held, sem):
        self.held, self.copy, self.open = held, pltpu.make_async_copy(held, target, sem), True

    def __setitem__(self, at, value):
        self.held[at] = value

    def flush(self):
        self.open = False
        self.copy.start()


def cost_of(microseconds):
    return pl.CostEstimate(
        flops=1 + microseconds * 10**9, bytes_accessed=1 + microseconds * 10**6 * 3, transcendentals=0
    )


def call(body, outs, args, scratch=(), vmem=32, beside=0):
    specs, arrays, extra = [], [], []
    for arg in args:
        if isinstance(arg, Scalars):
            specs.append(pl.BlockSpec(memory_space=pltpu.SMEM))
            arrays.append(arg.array)
        elif isinstance(arg, Far):
            specs.append(pl.BlockSpec(memory_space=pltpu.HBM))
            arrays.append(pltpu.with_memory_space_constraint(arg.array, pltpu.HBM))
            extra.append(pltpu.VMEM(arg.array.shape, arg.array.dtype))
            extra.append(pltpu.SemaphoreType.DMA((arg.parts,)))
        else:
            specs.append(pl.BlockSpec(memory_space=pltpu.VMEM))
            arrays.append(arg.array if isinstance(arg, JoinedHere) else arg)
    for shape, own in outs:
        if own:
            extra.append(pltpu.VMEM(shape, BF))
            extra.append(pltpu.SemaphoreType.DMA)

    def kernel(*refs):
        ins, rest = list(refs[: len(specs)]), refs[len(specs) :]
        targets, rest = rest[: len(outs)], rest[len(outs) :]
        buffers, rest = rest[: len(scratch)], list(rest[len(scratch) :])
        given = []
        for arg in args:
            ref = ins.pop(0)
            if isinstance(arg, Far):
                given.append(Fetched(ref, rest.pop(0), rest.pop(0), arg.parts))
            else:
                given.append(Rows(ref) if isinstance(arg, JoinedHere) else ref)
        kept = []
        for (_, own), ref in zip(outs, targets):
            kept.append(Kept(ref, rest.pop(0), rest.pop(0)) if own else ref)
        body(*given, *kept, *buffers)
        for held in kept:
            if isinstance(held, Kept):
                if held.open:
                    held.flush()
                held.copy.wait()
        for held in given:
            if isinstance(held, Fetched):
                for n in sorted(held.waiting):
                    held.copies[n].wait()

    return pl.pallas_call(
        kernel,
        out_shape=[
            pltpu.HBM(shape, BF) if own else jax.ShapeDtypeStruct(shape, BF) for shape, own in outs
        ],
        in_specs=specs,
        out_specs=[
            pl.BlockSpec(memory_space=pltpu.HBM if own else pltpu.VMEM) for _, own in outs
        ],
        scratch_shapes=list(scratch) + extra,
        compiler_params=pltpu.CompilerParams(vmem_limit_bytes=vmem * MIB),
        cost_estimate=cost_of(beside),
    )(*arrays)


def fetch_early(*arrays):
    def kernel(*refs):
        count = len(arrays)
        copies = []
        for n, arg in enumerate(arrays):
            source, target, sems = refs[n], refs[count + n], refs[2 * count + n]
            if isinstance(arg, Quarters):
                parts = [(source.at[:, arg.first + t], target.at[t]) for t in range(arg.count)]
            else:
                size = source.shape[0] // 4
                spans = [pl.ds(t * size, size) for t in range(4)]
                parts = [(source.at[span], target.at[span]) for span in spans]
            for t, (part, place) in enumerate(parts):
                copies.append(pltpu.make_async_copy(part, place, sems.at[t]))
                copies[-1].start()
        for copy in copies:
            copy.wait()

    shapes = [
        (v.count, 4, *v.array.shape[2:]) if isinstance(v, Quarters) else v.array.shape for v in arrays
    ]
    outs = pl.pallas_call(
        kernel,
        out_shape=[pltpu.VMEM(shape, BF) for shape in shapes],
        in_specs=[pl.BlockSpec(memory_space=pltpu.HBM)] * len(arrays),
        out_specs=[pl.BlockSpec(memory_space=pltpu.VMEM)] * len(arrays),
        scratch_shapes=[pltpu.SemaphoreType.DMA((4,))] * len(arrays),
        compiler_params=pltpu.CompilerParams(vmem_limit_bytes=4 * MIB),
        cost_estimate=cost_of(4),
    )(*[pltpu.with_memory_space_constraint(v.array, pltpu.HBM) for v in arrays])
    return list(outs)


def turn(w, out):
    row = lax.broadcasted_iota(jnp.int32, (128, 128), 0)
    column = lax.broadcasted_iota(jnp.int32, (128, 128), 1)
    pick = (row == column).astype(BF)
    for j in range(8):
        out[:, j * 512 : (j + 1) * 512] = nt(pick, w[j * 512 : (j + 1) * 512]).astype(BF)


def fine_forward(x, left, right, to_window, half, to_merge, gain, w, mgain, mw, fine, mid, own, far):
    xo = nn(to_window[...], x[...])
    xh = jnp.concatenate([nn(half[...], left[...]), nn(half[...], right[...])], axis=0)
    packs = []
    for value, kept in ((xo, own), (xh, far)):
        (unit,), _ = norm_parts([value])
        normed = (unit * gain[...]).astype(BF)
        pack = [rounded(nn(normed, w[t])) for t in range(3)]
        for t in range(3):
            kept[t] = pack[t].astype(BF)
        kept.flush()
        packs.append(pack)
    rows = []
    for at in range(0, T0, 72):
        parts = []
        for ch in range(0, C0, GROUP):
            q = packs[0][0][at : at + 72, ch : ch + GROUP]
            k, v = [
                jnp.concatenate([pk[t][at : at + 72, ch : ch + GROUP] for pk in packs], axis=0)
                for t in (1, 2)
            ]
            parts.append(mix(q, k, v))
        rows.append(jnp.concatenate(parts, axis=1))
    mixed = jnp.concatenate(rows, axis=0)
    out = rounded(xo + nt(mixed, w[3]))
    merged = nn(to_merge[...], out)
    fine[...] = merged.astype(BF)
    units, _ = norm_parts([merged[s * 72 : (s + 1) * 72] for s in range(4)])
    total = 0.0
    for s in range(4):
        span = slice(s * C0, (s + 1) * C0)
        total = total + nn(units[s] * mgain[:, span], mw[span])
    mid[...] = total.astype(BF)


def heads_of(w, g, t):
    return jnp.concatenate([w[4 * g + h, t] for h in range(4)], axis=0)


def middle_forward(x, partner, gain, w, rgain, out, packed, reduced, buf):
    own = x[...].astype(F32)
    both = jnp.concatenate([own, partner[...].astype(F32)], axis=0)
    (unit,), _ = norm_parts([both])
    normed = (unit * gain[...]).astype(BF)
    total = own
    for g in range(4):
        span = slice(g * GROUP, (g + 1) * GROUP)
        pack = [rounded(nt(normed, heads_of(w, g, t))) for t in range(3)]
        for t in range(3):
            packed[t, :, span] = pack[t].astype(BF)
        total = total + nn(mix(pack[0][:T1], pack[1], pack[2]), heads_of(w, g, 3))
    out[...] = total.astype(BF)
    buf[...] = rounded(total)
    units, _ = norm_parts([buf[s * T2 : (s + 1) * T2] for s in range(4)])
    reduced[...] = jnp.zeros_like(reduced)
    for s in range(4):
        span = slice(s * C1, (s + 1) * C1)
        reduced[:T2, span] = (units[s] * rgain[:, span]).astype(BF)


def below(parts):
    return jnp.concatenate([part[...] for part in parts], axis=0)


def halves_out(value, even, odd):
    even[...] = value[: 4 * PAD].astype(BF)
    odd[...] = value[4 * PAD :].astype(BF)


def coarse_reduce(chips, mates, own, other, out):
    tokens = below((chips, mates))
    out[:, :128] = nn(tokens, own[...]).astype(BF)
    out[:, 128:] = nn(tokens, other[...]).astype(BF)


def dead_keys():
    return lax.broadcasted_iota(jnp.int32, (8 * PAD, 1), 0) % PAD >= T2


def coarse_heads(own, others, t):
    return jnp.concatenate([own[t], others[t]], axis=1)


def coarse_forward(where, chips, mates, gain, own, others, even, odd, packed, kept, buf):
    for e, source in enumerate((chips, mates)):
        for d in range(4):
            columns = source[d * 8 * PAD : (d + 1) * 8 * PAD].astype(F32)
            for at in range(8):
                rows = columns[at * PAD : (at + 1) * PAD]
                to = ((at // 4 ^ e) * 4 + (at % 4 ^ d)) * PAD
                for r in range(2):
                    buf[where[d] ^ (2 * r + e), to : to + PAD] = rows[:, r * 128 : (r + 1) * 128]
    pieces = [buf[n] for n in range(16)]
    units, _ = norm_parts(pieces)
    normed = []
    for n in range(16):
        lanes = slice(n * 128, (n + 1) * 128)
        kept[:, lanes] = pieces[n][:PAD].astype(BF)
        normed.append((units[n] * gain[:, lanes]).astype(BF))
    normed = jnp.concatenate(normed, axis=1)
    pack = [rounded(nn(normed, coarse_heads(own, others, t))) for t in range(3)]
    for t in range(3):
        packed[t] = pack[t].astype(BF)
    mixed = mix(pack[0], pack[1], pack[2], dead_keys())
    halves_out(nt(mixed, coarse_heads(own, others, 3)), even, odd)


def total_of(parts):
    return sum(p[...].astype(F32) for p in parts)


def coarse_finish(a, b, c, d, x, gain, out, normed):
    value = rounded(x[...].astype(F32) + total_of((a, b, c, d)))
    out[...] = value.astype(BF)
    (unit,), _ = norm_parts([value])
    normed[...] = (unit * gain[...]).astype(BF)


def shards_of(own, other):
    return jnp.concatenate([own[...], other[0], other[1]], axis=1)


def lift_forward(chips, mates, own, other, even, odd):
    tokens = below((chips, mates))
    columns = nn(tokens, shards_of(own, other))
    halves_out(columns, even, odd)


def sens_back(sens, to_merge, ww, merged, grad):
    value = nn(to_merge[...], sens[...])
    merged[...] = value.astype(BF)
    total = 0.0
    for s in range(4):
        total = total + nt(value[s * 72 : (s + 1) * 72], ww[:, s * C0 : (s + 1) * C0])
    grad[...] = total.astype(BF)


def member_lanes(where, k, e, r):
    return pl.multiple_of((where[4 + k] % 4 ^ (2 * r + e)) * 256, 256)


def turn_point(
    where, a, b, c, d, mid, fine, grad, gain, ww, to_nat, out, joined_grad, even, odd, wide, flat
):
    for k, source in enumerate((a, b, c, d)):
        block = source[...].astype(F32)
        for e in range(2):
            rows = block[e * PAD : e * PAD + T2]
            for r in range(2):
                wide[where[4 + k] // 4, :, pl.ds(member_lanes(where, k, e, r), 256)] = rows[
                    :, r * 256 : (r + 1) * 256
                ]
    for s in range(4):
        flat[s * T2 : (s + 1) * T2] = wide[s]
    joined = rounded(mid[...].astype(F32) + flat[...])
    (unit,), scale = norm_parts([joined])
    normed = (unit * gain[...]).astype(BF)
    (back,) = norm_back([unit], scale, [grad[...].astype(F32) * gain[...]])
    joined_grad[...] = back.astype(BF)
    flat[...] = rounded(back)
    for s in range(4):
        wide[s] = flat[s * T2 : (s + 1) * T2]
    for e, target in enumerate((even, odd)):
        target[...] = jnp.zeros_like(target)
        for k in range(4):
            for r in range(2):
                target[k * PAD : k * PAD + T2, r * 256 : (r + 1) * 256] = wide[
                    where[4 + k] // 4, :, pl.ds(member_lanes(where, k, e, r), 256)
                ].astype(BF)
    rows = [
        fine[s * 72 : (s + 1) * 72].astype(F32) + nn(normed, ww[:, s * C0 : (s + 1) * C0])
        for s in range(4)
    ]
    out[...] = nn(to_nat[...], jnp.concatenate(rows, axis=0)).astype(BF)


def lift_back(a, b, c, d, own, other, even, odd):
    blocks = [v[...].astype(F32) for v in (a, b, c, d)]
    tokens = jnp.concatenate([v[:PAD] for v in blocks] + [v[PAD:] for v in blocks], axis=0)
    halves_out(nt(tokens, shards_of(own, other)), even, odd)


def coarse_out_back(a, b, c, d, value, gain, out):
    (unit,), scale = norm_parts([value[...].astype(F32)])
    cot = rounded(total_of((a, b, c, d))) * gain[...]
    out[...] = norm_back([unit], scale, [cot])[0].astype(BF)


def coarse_weights(packed, out):
    out[...] = weights_of(packed[0].astype(F32), packed[1].astype(F32), dead_keys()).astype(BF)


def coarse_back(chips, mates, packed, weights, own, others, even, odd):
    grad = rounded(nn(below((chips, mates)), coarse_heads(own, others, 3)))
    pack = [packed[t].astype(F32) for t in range(3)]
    grads = mix_back(pack[0], pack[1], pack[2], grad, weights[...])
    halves_out(sum(nt(grads[t], coarse_heads(own, others, t)) for t in range(3)), even, odd)


def coarse_in_back(a, b, c, d, value, gain, grad, w, out):
    (unit,), scale = norm_parts([value[...].astype(F32)])
    cot = rounded(total_of((a, b, c, d))) * gain[...]
    cot = (grad[...].astype(F32) + norm_back([unit], scale, [cot])[0]).astype(BF)
    total = 0.0
    for n in range(8):
        total = total + nn(cot[:, n * 256 : (n + 1) * 256], w[2 * n : 2 * n + 2].reshape(256, -1))
    out[...] = total.astype(BF)


def middle_out_back(cots, mid, gain, grad, out, buf, back):
    buf[...] = mid[...].astype(F32)
    units, scale = norm_parts([buf[s * T2 : (s + 1) * T2] for s in range(4)])
    cot = cots[:T2].astype(F32) * gain[...]
    backs = norm_back(units, scale, [cot[:, s * C1 : (s + 1) * C1] for s in range(4)])
    for s in range(4):
        back[s * T2 : (s + 1) * T2] = backs[s]
    out[...] = (grad[...].astype(F32) + back[...]).astype(BF)


def middle_weights(packed, out):
    for g in range(4):
        span = slice(g * GROUP, (g + 1) * GROUP)
        q, k = [packed[t, :, span].astype(F32) for t in range(2)]
        out[g] = weights_of(q, k).astype(BF)


def middle_back(grad, partner, x, packed, weights, gain, w, fine, sens, mgain, mw, to_window, out):
    own = grad[...].astype(F32)
    both = jnp.concatenate([own, partner[...].astype(F32)], axis=0)
    total = 0.0
    for g in range(4):
        span = slice(g * GROUP, (g + 1) * GROUP)
        mixed = rounded(nt(both, heads_of(w, g, 3)))
        pack = [packed[t, :, span].astype(F32) for t in range(3)]
        grads = mix_back(pack[0], pack[1], pack[2], mixed, weights[g])
        for t in range(3):
            total = total + nn(grads[t][:T1], heads_of(w, g, t))
    (unit,), scale = norm_parts([x[...].astype(F32)])
    into = (own + norm_back([unit], scale, [rounded(total) * gain[...]])[0]).astype(BF)
    units, scale = norm_parts([fine[s * 72 : (s + 1) * 72].astype(F32) for s in range(4)])
    cots = []
    for s in range(4):
        span = slice(s * C0, (s + 1) * C0)
        cots.append(rounded(nt(into, mw[span])) * mgain[:, span])
    backs = jnp.concatenate(norm_back(units, scale, cots), axis=0)
    out[...] = nn(to_window[...], sens[...].astype(F32) + backs).astype(BF)


def window_pack(own, far, at, ch, t):
    span, lanes = slice(at, at + 72), slice(ch, ch + GROUP)
    return jnp.concatenate([own[t, span, lanes].astype(F32), far[t, span, lanes].astype(F32)], axis=0)


def fine_weights(grad, own, far, w, mixed, out):
    mixed[...] = nn(grad[...], w[0]).astype(BF)
    for n, at in enumerate(range(0, T0, 72)):
        for g, ch in enumerate(range(0, C0, GROUP)):
            q, k = [window_pack(own, far, at, ch, t) for t in range(2)]
            out[2 * n + g] = weights_of(q, k).astype(BF)


def fine_back(
    grad, left, right, mixed, weights, own, far, x, to_window, to_nat, gain, w, out
):
    go = grad[...]
    mixed_own = mixed[...].astype(F32)
    mixed_far = jnp.concatenate([rounded(nn(v[...], w[3])) for v in (left, right)], axis=0)
    rows = [[], [], []]
    for n, at in enumerate(range(0, T0, 72)):
        parts = [[], [], []]
        for g, ch in enumerate(range(0, C0, GROUP)):
            span, lanes = slice(at, at + 72), slice(ch, ch + GROUP)
            pack = [window_pack(own, far, at, ch, t) for t in range(3)]
            both = jnp.concatenate([mixed_own[span, lanes], mixed_far[span, lanes]], axis=0)
            grads = mix_back(pack[0], pack[1], pack[2], both, weights[2 * n + g])
            for t in range(3):
                parts[t].append(grads[t][:72])
        for t in range(3):
            rows[t].append(jnp.concatenate(parts[t], axis=1))
    total = sum(nt(jnp.concatenate(rows[t], axis=0), w[t]) for t in range(3))
    (unit,), scale = norm_parts([nn(to_window[...], x[...])])
    back = go.astype(F32) + norm_back([unit], scale, [rounded(total) * gain[...]])[0]
    out[...] = nn(to_nat[...], back).astype(BF)


def local(
    latent_field,
    sensitivity,
    first_gain,
    first_proj,
    merge_gain,
    merge_weight,
    middle_gain,
    middle_proj,
    reduce_gain,
    reduce_weight,
    coarse_gain,
    coarse_proj,
    lift_gain,
    lift_weight,
    widen_gain,
    widen_weight,
):
    lat, lon = lax.axis_index("lat"), lax.axis_index("lon")
    places = [jnp.asarray(table(rule))[lat % 2, lon] for rule in (fellow, member_of)]
    where = Scalars(jnp.concatenate(places))

    def row(gain):
        return Far(gain.reshape(1, -1))

    def flat(field):
        return field.transpose(0, 2, 1, 3).reshape(T0, C0)

    def unflat(tokens):
        return tokens.reshape(12, 12, 2, C0).transpose(0, 2, 1, 3)

    mid_w = lax.all_gather(middle_proj.transpose(0, 2, 1), "lon", axis=0)
    x = flat(latent_field)
    from_left = send(x[144:], RIGHT)
    from_right = send(x[:144], LEFT)
    reduce_other = send(reduce_weight, NEAR)
    size = C2 // 4

    def quarter(shard, axis):
        return lax.dynamic_slice_in_dim(shard, lat // 2 * size, size, axis)

    lift_part = quarter(lift_weight, 0)
    bundle = send(
        jnp.concatenate([quarter(coarse_proj, 1), lift_part[None, :, :128], lift_part[None, :, 128:]]),
        NEAR,
    )

    def early(start, *operands):
        arrays = after(start, *(v.array for v in operands))[1:]
        return fetch_early(*(v.with_array(array) for v, array in zip(operands, arrays)))

    def order(matrix):
        return Far(jnp.asarray(matrix, BF))

    x, reduce_other = after(x, reduce_other)
    reduce_w = (Far(reduce_weight), Far(reduce_other))
    fine, mid_in, own, far = call(
        fine_forward,
        [((T0, C0), False), ((T1, C1), False), ((3, T0, C0), True), ((3, T0, C0), True)],
        (x, from_left, from_right, order(TO_WINDOW), order(HALF_WINDOW), order(WINDOW_TO_MERGE),
         row(first_gain), Far(first_proj, 4), row(merge_gain), Far(merge_weight, 4)),
    )
    sens, sens_grad = call(
        sens_back,
        [((T0, C0), False), ((T1, C1), False)],
        (flat(sensitivity), order(TO_MERGE), Far(widen_weight)),
    )
    mid_in, bundle = after(mid_in, bundle)
    mid_far = send(mid_in, HALF)
    reduce_later, _ = after(reduce_weight, mid_in)
    (reduce_turned,) = call(turn, [((128, 4 * C1), False)], (Far(reduce_later),))
    others = lax.all_gather(
        bundle, "lat", axis_index_groups=[[p, p + 2, p + 4, p + 6] for p in range(2)], axis=0
    )
    coarse_w = (Far(coarse_proj, 4), Quarters(others, 0, 4))
    lift_w = (Far(lift_weight), Quarters(others, 4, 2))
    mid_far, sens, sens_grad = after(mid_far, sens, sens_grad)
    mid, mid_packed, reduced = call(
        middle_forward,
        [((T1, C1), False), ((3, 2 * T1, C1), True), ((PAD, 4 * C1), False)],
        (mid_in, mid_far, row(middle_gain), Far(mid_w, 4), row(reduce_gain)),
        scratch=[pltpu.VMEM((T1, C1), F32)],
    )
    later, _ = after(reduce_turned, mid)
    reduce_all = lax.all_gather(later, "lon", axis=0)
    rows = 8 * PAD
    near = early(reduced, *reduce_w)
    tokens, near = to_ring(reduced, *near)
    (columns_in,) = call(coarse_reduce, [((rows, 256), False)], (*tokens, *near))


    def halves(width):
        return [((4 * PAD, width), False), ((4 * PAD, width), False)]

    tokens, near = gather8(columns_in, *early(columns_in, *coarse_w))
    even, odd, coarse_packed, coarse_in = call(
        coarse_forward,
        halves(C2) + [((3, rows, 256), False), ((PAD, C2), False)],
        (where, *tokens, row(coarse_gain), near[0], JoinedHere(near[1])),
        scratch=[pltpu.VMEM((16, rows, 128), F32)],
    )
    coarse_out, lift_in = call(
        coarse_finish,
        [((PAD, C2), False), ((PAD, C2), False)],
        (*scatter8(even, odd), coarse_in, row(lift_gain)),
    )
    tokens, near = gather8(lift_in, *early(lift_in, *lift_w))
    even, odd = call(lift_forward, halves(512), (*tokens, near[0], JoinedHere(near[1])))
    (widen_near,) = early(even, Far(widen_weight))
    predicted, joined_grad, even, odd = call(
        turn_point,
        [((T0, C0), False), ((T1, C1), False)] + halves(512),
        (where, *exchange8(even, odd, BACK), mid, Far(fine), Far(sens_grad), row(widen_gain),
         widen_near, order(TO_MERGE.T)),
        scratch=[pltpu.VMEM((4, T2, C1), F32), pltpu.VMEM((T1, C1), F32)],
    )
    near = early(even, *lift_w)
    even, odd = call(
        lift_back, halves(C2), (*exchange8(even, odd, OUT), near[0], JoinedHere(near[1]))
    )
    (coarse_grad,) = call(
        coarse_out_back, [((PAD, C2), False)], (*scatter8(even, odd), coarse_out, row(lift_gain))
    )
    packed, _ = after(coarse_packed, coarse_grad)
    (soft,) = call(coarse_weights, [((rows, 4 * rows), False)], (Far(packed),), beside=4)
    tokens, near = gather8(coarse_grad, soft, *early(coarse_grad, *coarse_w))
    even, odd = call(
        coarse_back,
        halves(C2),
        (*tokens, Far(coarse_packed), near[0], near[1], JoinedHere(near[2])),
    )
    (reduce_near,) = early(even, Far(reduce_all))
    (reduced_grad,) = call(
        coarse_in_back,
        [((PAD, 4 * C1), False)],
        (*scatter8(even, odd), coarse_in, row(coarse_gain), coarse_grad, reduce_near),
        vmem=16,
    )
    (mid_grad,) = call(
        middle_out_back,
        [((T1, C1), False)],
        (send(reduced_grad, BACK[0]), mid, row(reduce_gain), joined_grad),
        scratch=[pltpu.VMEM((T1, C1), F32), pltpu.VMEM((T1, C1), F32)],
    )
    packed, mid_w, merge_weight, _ = after(mid_packed, mid_w, merge_weight, reduced_grad)
    (mid_soft,) = call(middle_weights, [((4, 2 * T1, 8 * T1), False)], (Far(packed),), vmem=16, beside=4)
    mid_near, merge_near = fetch_early(Far(mid_w), Far(merge_weight))
    (fine_grad,) = call(
        middle_back,
        [((T0, C0), False)],
        (mid_grad, send(mid_grad, HALF), mid_in, Far(mid_packed), mid_soft, row(middle_gain),
         mid_near, Far(fine), Far(sens), row(merge_gain), merge_near, order(WINDOW_TO_MERGE.T)),
    )
    grad_left = send(fine_grad[144:], RIGHT)
    grad_right = send(fine_grad[:144], LEFT)
    own, far, _ = after(own, far, fine_grad)
    mixed, fine_soft = call(
        fine_weights,
        [((T0, C0), False), ((8, 2 * T1, 8 * T1), False)],
        (fine_grad, Far(own), Far(far), Far(first_proj[3:])),
        beside=6,
    )
    (result,) = call(
        fine_back,
        [((T0, C0), False)],
        (fine_grad, grad_left, grad_right, mixed, fine_soft, Far(own), Far(far), Far(x),
         order(TO_WINDOW), order(TO_WINDOW.T), row(first_gain), Far(first_proj, 4)),
    )
    return unflat(predicted), unflat(result)


def solution(mesh):
    field = P("lon", None, "lat", None)
    placed = (
        field, field, P(), P(), P(), P(), P(), P(None, None, "lon"), P(), P(None, "lon"), P(),
        P(None, None, "lon"), P(), P(None, "lon"), P(), P(),
    )
    return jax.shard_map(
        local, mesh=mesh, in_specs=placed, out_specs=(field, field), check_vma=False
    )
```

```python
import jax
import jax.numpy as jnp
import numpy as np
from jax import lax
from jax.experimental import pallas as pl
from jax.experimental.pallas import tpu as pltpu
from jax.sharding import PartitionSpec as P

BF = jnp.bfloat16
F32 = jnp.float32
EPSILON = 1e-05
HD = 64
GROUP = 4 * HD
LAT, LON = 8, 16
AXES = ("lat", "lon")
T0, T1, T2 = 288, 72, 18
PAD = 24
C0, C1, C2 = 512, 1024, 2048
MIB = 1024 * 1024


def orders():
    window, merge = {}, {}
    for c in range(12):
        for lev in range(2):
            for r in range(12):
                nat = (c * 12 + r) * 2 + lev
                cw, ci, b = c // 6, c % 6 // 2, c % 2
                rw, rj, a = r // 6, r % 6 // 2, r % 2
                s = 2 * a + b
                window[nat] = (cw * 2 + rw) * 72 + s * 18 + (ci * 2 + lev) * 3 + rj
                mc, mr = c // 2, r // 2
                s1 = 2 * (mr % 2) + mc % 2
                merge[nat] = s * 72 + s1 * 18 + (mc // 2 * 2 + lev) * 3 + mr // 2
    to_window = np.zeros((T0, T0), np.float32)
    to_merge = np.zeros((T0, T0), np.float32)
    for nat in range(T0):
        to_window[window[nat], nat] = 1
        to_merge[merge[nat], nat] = 1
    half = np.zeros((144, 144), np.float32)
    for nat in range(144):
        half[window[nat], nat] = 1
    return to_window, half, to_merge


TO_WINDOW, HALF_WINDOW, TO_MERGE = orders()
WINDOW_TO_MERGE = TO_MERGE @ TO_WINDOW.T


ALONG = (0, 1, 3, 2)


def number(lat, lon):
    return lat % LAT * LON + lon % LON


def pairs_of(rule):
    return [(number(a, i), number(*rule(a, i))) for a in range(LAT) for i in range(LON)]


def member_of(lat, lon, k):
    shifted = (lon - 2) % LON
    which = (2 * (lat % 2) + shifted % 4 // 2) ^ k
    return (
        lat // 2 * 2 + which // 2,
        4 * ((shifted // 4 + ALONG[which]) % 4) + 2 * (1 - which % 2) + lon % 2,
    )


def fellow(lat, lon, k):
    which = 2 * (lat % 2) + 1 - lon // 2 % 2
    window = (lon // 4 - ALONG[which]) % 4
    which ^= k
    return (
        lat // 2 * 2 + which // 2,
        4 * ((window + ALONG[which]) % 4) + 2 * (1 - which % 2) + lon % 2,
    )


def table(rule):
    return np.array(
        [[[rule(a, i, k)[1] for k in range(4)] for i in range(LON)] for a in range(2)], np.int32
    )


OUT = [pairs_of(lambda a, i, k=k: member_of(a, i, k)) for k in range(4)]
BACK = [[(target, source) for source, target in pairs] for pairs in OUT]
RING = [pairs_of(lambda a, i, k=k: fellow(a, i, k)) for k in range(4)]
CORE = pairs_of(lambda a, i: (a, i ^ 1))
NEAR = pairs_of(lambda a, i: (a ^ 1, i ^ 2))
RIGHT = pairs_of(lambda a, i: (a, i + 1))
LEFT = pairs_of(lambda a, i: (a, i - 1))
HALF = pairs_of(lambda a, i: (a, i + 1 if i % 2 else i - 1))


def send(value, pairs):
    return lax.ppermute(value, AXES, pairs)


def after(value, *others):
    return lax.optimization_barrier((value, *others))


def across(parts, meanwhile):
    chips, *meanwhile = after(jnp.concatenate(parts), *meanwhile)
    return (chips, send(chips, CORE)), meanwhile


def to_ring(block, *meanwhile):
    return across([send(block, OUT[k]) for k in range(4)], meanwhile)


def gather8(block, *meanwhile):
    return across([block] + [send(block, RING[k]) for k in (1, 2, 3)], meanwhile)


def chip_sums(even, odd):
    both = (even.astype(F32) + send(odd, CORE).astype(F32)).astype(BF)
    return [both[k * PAD : (k + 1) * PAD] for k in range(4)]


def scatter8(even, odd):
    parts = chip_sums(even, odd)
    return [parts[0]] + [send(parts[k], RING[k]) for k in (1, 2, 3)]


def scatter_back(even, odd):
    return [send(part, BACK[k]) for k, part in enumerate(chip_sums(even, odd))]


def exchange8(even, odd, ways):
    other = send(odd, CORE)
    return [
        send(jnp.concatenate([even[k * PAD : (k + 1) * PAD], other[k * PAD : (k + 1) * PAD]]), ways[k])
        for k in range(4)
    ]


def nn(a, b):
    return lax.dot_general(
        a.astype(BF), b.astype(BF), (((1,), (0,)), ((), ())), preferred_element_type=F32
    )


def nt(a, b):
    return lax.dot_general(
        a.astype(BF), b.astype(BF), (((1,), (1,)), ((), ())), preferred_element_type=F32
    )


def tn(a, b):
    return lax.dot_general(
        a.astype(BF), b.astype(BF), (((0,), (0,)), ((), ())), preferred_element_type=F32
    )


def rounded(value):
    return value.astype(BF).astype(F32)


def norm_parts(pieces):
    width = sum(v.shape[1] for v in pieces)
    mean = sum(jnp.sum(v, axis=1, keepdims=True) for v in pieces) / width
    centred = [v - mean for v in pieces]
    spread = sum(jnp.sum(v * v, axis=1, keepdims=True) for v in centred) / width
    scale = lax.rsqrt(spread + EPSILON)
    return [v * scale for v in centred], scale


def norm_back(unit, scale, cot):
    width = sum(v.shape[1] for v in unit)
    first = sum(jnp.sum(v, axis=1, keepdims=True) for v in cot) / width
    second = sum(jnp.sum(v * u, axis=1, keepdims=True) for v, u in zip(cot, unit)) / width
    return [scale * (v - first - u * second) for v, u in zip(cot, unit)]


def head_masks():
    lane = lax.broadcasted_iota(jnp.int32, (1, GROUP), 1) // HD
    return [(lane == h).astype(F32) for h in range(4)]


def by_head(value):
    return jnp.concatenate([value * m for m in head_masks()], axis=0)


def own_heads(value, rows):
    return sum(value[h * rows : (h + 1) * rows] * m for h, m in enumerate(head_masks()))


def weights_of(q, k, dead=None):
    scores = nt(k, by_head(q)) * HD ** (-0.5)
    if dead is not None:
        scores = jnp.where(dead, -1e30, scores)
    raised = jnp.exp(scores - jnp.max(scores, axis=0, keepdims=True))
    return raised / jnp.sum(raised, axis=0, keepdims=True)


def mix(weights, v, rows):
    return rounded(own_heads(tn(weights, v), rows))


def mix_back(q, k, v, grad, weights):
    grads = by_head(grad)
    from_weights = nt(v, grads)
    soft = weights.astype(F32)
    inner = jnp.sum(soft * from_weights, axis=0, keepdims=True)
    from_scores = soft * (from_weights - inner) * HD ** (-0.5)
    return (
        rounded(own_heads(tn(from_scores, k), q.shape[0])),
        rounded(nn(from_scores, by_head(q))),
        rounded(nn(weights, grads)),
    )


class Scalars:
    def __init__(self, array):
        self.array = array


class Far:
    def __init__(self, array, parts=1):
        self.array, self.parts = array, parts

    def with_array(self, array):
        return Far(array, self.parts)


class Quarters:
    def __init__(self, array, first, count):
        self.array, self.first, self.count = array, first, count

    def with_array(self, array):
        return Quarters(array, self.first, self.count)


class JoinedHere:
    def __init__(self, array):
        self.array = array


class Rows:
    def __init__(self, ref):
        self.ref = ref

    def __getitem__(self, t):
        value = self.ref[t]
        return value.reshape(-1, value.shape[-1])


class Fetched:
    def __init__(self, source, held, sems, parts):
        self.held, self.size = held, source.shape[0] // parts
        self.copies = [
            pltpu.make_async_copy(
                source.at[pl.ds(n * self.size, self.size)],
                held.at[pl.ds(n * self.size, self.size)],
                sems.at[n],
            )
            for n in range(parts)
        ]
        for copy in self.copies:
            copy.start()
        self.waiting = set(range(parts))

    def __getitem__(self, at):
        lead = at[0] if isinstance(at, tuple) else at
        if isinstance(lead, int):
            wanted = {lead // self.size}
        elif isinstance(lead, slice):
            first, last, _ = lead.indices(self.held.shape[0])
            wanted = set(range(first // self.size, (last - 1) // self.size + 1))
        else:
            wanted = set(self.waiting)
        for n in sorted(wanted & self.waiting):
            self.copies[n].wait()
        self.waiting -= wanted
        return self.held[at]


class Kept:
    def __init__(self, target, held, sem):
        self.held, self.copy, self.open = held, pltpu.make_async_copy(held, target, sem), True

    def __setitem__(self, at, value):
        self.held[at] = value

    def flush(self):
        self.open = False
        self.copy.start()


def cost_of(microseconds):
    return pl.CostEstimate(
        flops=1 + microseconds * 10**9, bytes_accessed=1 + microseconds * 10**6 * 3, transcendentals=0
    )


def call(body, outs, args, scratch=(), vmem=24, beside=0):
    specs, arrays, extra = [], [], []
    for arg in args:
        if isinstance(arg, Scalars):
            specs.append(pl.BlockSpec(memory_space=pltpu.SMEM))
            arrays.append(arg.array)
        elif isinstance(arg, Far):
            specs.append(pl.BlockSpec(memory_space=pltpu.HBM))
            arrays.append(pltpu.with_memory_space_constraint(arg.array, pltpu.HBM))
            extra.append(pltpu.VMEM(arg.array.shape, arg.array.dtype))
            extra.append(pltpu.SemaphoreType.DMA((arg.parts,)))
        else:
            specs.append(pl.BlockSpec(memory_space=pltpu.VMEM))
            arrays.append(arg.array if isinstance(arg, JoinedHere) else arg)
    for shape, own in outs:
        if own:
            extra.append(pltpu.VMEM(shape, BF))
            extra.append(pltpu.SemaphoreType.DMA)

    def kernel(*refs):
        ins, rest = list(refs[: len(specs)]), refs[len(specs) :]
        targets, rest = rest[: len(outs)], rest[len(outs) :]
        buffers, rest = rest[: len(scratch)], list(rest[len(scratch) :])
        given = []
        for arg in args:
            ref = ins.pop(0)
            if isinstance(arg, Far):
                given.append(Fetched(ref, rest.pop(0), rest.pop(0), arg.parts))
            else:
                given.append(Rows(ref) if isinstance(arg, JoinedHere) else ref)
        kept = []
        for (_, own), ref in zip(outs, targets):
            kept.append(Kept(ref, rest.pop(0), rest.pop(0)) if own else ref)
        body(*given, *kept, *buffers)
        for held in kept:
            if isinstance(held, Kept):
                if held.open:
                    held.flush()
                held.copy.wait()
        for held in given:
            if isinstance(held, Fetched):
                for n in sorted(held.waiting):
                    held.copies[n].wait()

    return pl.pallas_call(
        kernel,
        out_shape=[
            pltpu.HBM(shape, BF) if own else jax.ShapeDtypeStruct(shape, BF) for shape, own in outs
        ],
        in_specs=specs,
        out_specs=[
            pl.BlockSpec(memory_space=pltpu.HBM if own else pltpu.VMEM) for _, own in outs
        ],
        scratch_shapes=list(scratch) + extra,
        compiler_params=pltpu.CompilerParams(vmem_limit_bytes=vmem * MIB),
        cost_estimate=cost_of(beside),
    )(*arrays)


def fetch_early(*arrays):
    def kernel(*refs):
        count = len(arrays)
        copies = []
        for n, arg in enumerate(arrays):
            source, target, sems = refs[n], refs[count + n], refs[2 * count + n]
            if isinstance(arg, Quarters):
                parts = [(source.at[:, arg.first + t], target.at[t]) for t in range(arg.count)]
            else:
                size = source.shape[0] // 4
                spans = [pl.ds(t * size, size) for t in range(4)]
                parts = [(source.at[span], target.at[span]) for span in spans]
            for t, (part, place) in enumerate(parts):
                copies.append(pltpu.make_async_copy(part, place, sems.at[t]))
                copies[-1].start()
        for copy in copies:
            copy.wait()

    shapes = [
        (v.count, 4, *v.array.shape[2:]) if isinstance(v, Quarters) else v.array.shape for v in arrays
    ]
    outs = pl.pallas_call(
        kernel,
        out_shape=[pltpu.VMEM(shape, BF) for shape in shapes],
        in_specs=[pl.BlockSpec(memory_space=pltpu.HBM)] * len(arrays),
        out_specs=[pl.BlockSpec(memory_space=pltpu.VMEM)] * len(arrays),
        scratch_shapes=[pltpu.SemaphoreType.DMA((4,))] * len(arrays),
        compiler_params=pltpu.CompilerParams(vmem_limit_bytes=4 * MIB),
        cost_estimate=cost_of(4),
    )(*[pltpu.with_memory_space_constraint(v.array, pltpu.HBM) for v in arrays])
    return list(outs)


def turn(w, out):
    row = lax.broadcasted_iota(jnp.int32, (128, 128), 0)
    column = lax.broadcasted_iota(jnp.int32, (128, 128), 1)
    pick = (row == column).astype(BF)
    for j in range(8):
        out[:, j * 512 : (j + 1) * 512] = nt(pick, w[j * 512 : (j + 1) * 512]).astype(BF)


def fine_forward(x, left, right, to_window, half, to_merge, gain, w, mgain, mw, fine, mid, own, far):
    xo = nn(to_window[...], x[...])
    xh = jnp.concatenate([nn(half[...], left[...]), nn(half[...], right[...])], axis=0)
    packs = []
    for value, kept in ((xo, own), (xh, far)):
        (unit,), _ = norm_parts([value])
        normed = (unit * gain[...]).astype(BF)
        pack = [rounded(nn(normed, w[t])) for t in range(3)]
        for t in range(3):
            kept[t] = pack[t].astype(BF)
        kept.flush()
        packs.append(pack)
    rows = []
    for at in range(0, T0, 72):
        parts = []
        for ch in range(0, C0, GROUP):
            q = packs[0][0][at : at + 72, ch : ch + GROUP]
            k, v = [
                jnp.concatenate([pk[t][at : at + 72, ch : ch + GROUP] for pk in packs], axis=0)
                for t in (1, 2)
            ]
            parts.append(mix(weights_of(q, k), v, 72))
        rows.append(jnp.concatenate(parts, axis=1))
    mixed = jnp.concatenate(rows, axis=0)
    out = rounded(xo + nt(mixed, w[3]))
    merged = nn(to_merge[...], out)
    fine[...] = merged.astype(BF)
    units, _ = norm_parts([merged[s * 72 : (s + 1) * 72] for s in range(4)])
    total = 0.0
    for s in range(4):
        span = slice(s * C0, (s + 1) * C0)
        total = total + nn(units[s] * mgain[:, span], mw[span])
    mid[...] = total.astype(BF)


def heads_of(w, g, t):
    return jnp.concatenate([w[4 * g + h, t] for h in range(4)], axis=0)


def middle_forward(x, partner, gain, w, rgain, out, packed, reduced, buf):
    own = x[...].astype(F32)
    both = jnp.concatenate([own, partner[...].astype(F32)], axis=0)
    (unit,), _ = norm_parts([both])
    normed = (unit * gain[...]).astype(BF)
    total = own
    for g in range(4):
        span = slice(g * GROUP, (g + 1) * GROUP)
        pack = [rounded(nt(normed, heads_of(w, g, t))) for t in range(3)]
        for t in range(3):
            packed[t, :, span] = pack[t].astype(BF)
        total = total + nn(mix(weights_of(pack[0][:T1], pack[1]), pack[2], T1), heads_of(w, g, 3))
    out[...] = total.astype(BF)
    buf[...] = rounded(total)
    units, _ = norm_parts([buf[s * T2 : (s + 1) * T2] for s in range(4)])
    reduced[...] = jnp.zeros_like(reduced)
    for s in range(4):
        span = slice(s * C1, (s + 1) * C1)
        reduced[:T2, span] = (units[s] * rgain[:, span]).astype(BF)


def below(parts):
    return jnp.concatenate([part[...] for part in parts], axis=0)


def halves_out(value, even, odd):
    even[...] = value[: 4 * PAD].astype(BF)
    odd[...] = value[4 * PAD :].astype(BF)


def coarse_reduce(chips, mates, own, other, out):
    tokens = below((chips, mates))
    out[:, :128] = nn(tokens, own[...]).astype(BF)
    out[:, 128:] = nn(tokens, other[...]).astype(BF)


def dead_keys():
    return lax.broadcasted_iota(jnp.int32, (8 * PAD, 1), 0) % PAD >= T2


def coarse_heads(own, others, t):
    return jnp.concatenate([own[t], others[t]], axis=1)


def coarse_forward(where, chips, mates, gain, own, others, even, odd, packed, kept, soft, buf):
    for e, source in enumerate((chips, mates)):
        for d in range(4):
            columns = source[d * 8 * PAD : (d + 1) * 8 * PAD].astype(F32)
            for at in range(8):
                rows = columns[at * PAD : (at + 1) * PAD]
                to = ((at // 4 ^ e) * 4 + (at % 4 ^ d)) * PAD
                for r in range(2):
                    buf[where[d] ^ (2 * r + e), to : to + PAD] = rows[:, r * 128 : (r + 1) * 128]
    pieces = [buf[n] for n in range(16)]
    units, _ = norm_parts(pieces)
    normed = []
    for n in range(16):
        lanes = slice(n * 128, (n + 1) * 128)
        kept[:, lanes] = pieces[n][:PAD].astype(BF)
        normed.append((units[n] * gain[:, lanes]).astype(BF))
    normed = jnp.concatenate(normed, axis=1)
    pack = [rounded(nn(normed, coarse_heads(own, others, t))) for t in range(3)]
    for t in range(3):
        packed[t] = pack[t].astype(BF)
    weights = weights_of(pack[0], pack[1], dead_keys())
    soft[...] = weights.astype(BF)
    mixed = mix(weights, pack[2], 8 * PAD)
    halves_out(nt(mixed, coarse_heads(own, others, 3)), even, odd)


def total_of(parts):
    return sum(p[...].astype(F32) for p in parts)


def coarse_finish(a, b, c, d, x, gain, out, normed):
    value = rounded(x[...].astype(F32) + total_of((a, b, c, d)))
    out[...] = value.astype(BF)
    (unit,), _ = norm_parts([value])
    normed[...] = (unit * gain[...]).astype(BF)


def shards_of(own, other):
    return jnp.concatenate([own[...], other[0], other[1]], axis=1)


def lift_forward(chips, mates, own, other, even, odd):
    tokens = below((chips, mates))
    columns = nn(tokens, shards_of(own, other))
    halves_out(columns, even, odd)


def sens_back(sens, to_merge, ww, merged, grad):
    value = nn(to_merge[...], sens[...])
    merged[...] = value.astype(BF)
    total = 0.0
    for s in range(4):
        total = total + nt(value[s * 72 : (s + 1) * 72], ww[:, s * C0 : (s + 1) * C0])
    grad[...] = total.astype(BF)


def member_lanes(where, k, e, r):
    return pl.multiple_of((where[4 + k] % 4 ^ (2 * r + e)) * 256, 256)


def turn_point(
    where, a, b, c, d, mid, grad, gain, out, joined_grad, even, odd, wide, flat
):
    for k, source in enumerate((a, b, c, d)):
        block = source[...].astype(F32)
        for e in range(2):
            rows = block[e * PAD : e * PAD + T2]
            for r in range(2):
                wide[where[4 + k] // 4, :, pl.ds(member_lanes(where, k, e, r), 256)] = rows[
                    :, r * 256 : (r + 1) * 256
                ]
    for s in range(4):
        flat[s * T2 : (s + 1) * T2] = wide[s]
    joined = rounded(mid[...].astype(F32) + flat[...])
    (unit,), scale = norm_parts([joined])
    out[...] = (unit * gain[...]).astype(BF)
    (back,) = norm_back([unit], scale, [grad[...].astype(F32) * gain[...]])
    joined_grad[...] = back.astype(BF)
    flat[...] = rounded(back)
    for s in range(4):
        wide[s] = flat[s * T2 : (s + 1) * T2]
    for e, target in enumerate((even, odd)):
        target[...] = jnp.zeros_like(target)
        for k in range(4):
            for r in range(2):
                target[k * PAD : k * PAD + T2, r * 256 : (r + 1) * 256] = wide[
                    where[4 + k] // 4, :, pl.ds(member_lanes(where, k, e, r), 256)
                ].astype(BF)


def widen(normed, fine, ww, to_nat, out):
    rows = [
        fine[s * 72 : (s + 1) * 72].astype(F32) + nn(normed[...], ww[:, s * C0 : (s + 1) * C0])
        for s in range(4)
    ]
    out[...] = nn(to_nat[...], jnp.concatenate(rows, axis=0)).astype(BF)


def lift_back(a, b, c, d, own, other, even, odd):
    blocks = [v[...].astype(F32) for v in (a, b, c, d)]
    tokens = jnp.concatenate([v[:PAD] for v in blocks] + [v[PAD:] for v in blocks], axis=0)
    halves_out(nt(tokens, shards_of(own, other)), even, odd)


def coarse_out_back(a, b, c, d, value, gain, out):
    (unit,), scale = norm_parts([value[...].astype(F32)])
    cot = rounded(total_of((a, b, c, d))) * gain[...]
    out[...] = norm_back([unit], scale, [cot])[0].astype(BF)


def coarse_back(chips, mates, packed, weights, own, others, even, odd):
    grad = rounded(nn(below((chips, mates)), coarse_heads(own, others, 3)))
    pack = [packed[t].astype(F32) for t in range(3)]
    grads = mix_back(pack[0], pack[1], pack[2], grad, weights[...])
    halves_out(sum(nt(grads[t], coarse_heads(own, others, t)) for t in range(3)), even, odd)


def coarse_in_back(a, b, c, d, pair, gain, w, mid, mid_gain, mid_grad, out, buf, back):
    (unit,), scale = norm_parts([pair[:PAD].astype(F32)])
    cot = rounded(total_of((a, b, c, d))) * gain[...]
    cot = (pair[PAD:].astype(F32) + norm_back([unit], scale, [cot])[0]).astype(BF)
    total = 0.0
    for n in range(8):
        total = total + nn(cot[:, n * 256 : (n + 1) * 256], w[2 * n : 2 * n + 2].reshape(256, -1))
    buf[...] = mid[...].astype(F32)
    units, scale = norm_parts([buf[s * T2 : (s + 1) * T2] for s in range(4)])
    cot = rounded(total[:T2]) * mid_gain[...]
    backs = norm_back(units, scale, [cot[:, s * C1 : (s + 1) * C1] for s in range(4)])
    for s in range(4):
        back[s * T2 : (s + 1) * T2] = backs[s]
    out[...] = (mid_grad[...].astype(F32) + back[...]).astype(BF)


def middle_weights(packed, out):
    for g in range(4):
        span = slice(g * GROUP, (g + 1) * GROUP)
        q, k = [packed[t, :, span].astype(F32) for t in range(2)]
        out[g] = weights_of(q, k).astype(BF)


def middle_back(grad, partner, x, packed, weights, gain, w, fine, sens, mgain, mw, to_window, out):
    own = grad[...].astype(F32)
    both = jnp.concatenate([own, partner[...].astype(F32)], axis=0)
    total = 0.0
    for g in range(4):
        span = slice(g * GROUP, (g + 1) * GROUP)
        mixed = rounded(nt(both, heads_of(w, g, 3)))
        pack = [packed[t, :, span].astype(F32) for t in range(3)]
        grads = mix_back(pack[0], pack[1], pack[2], mixed, weights[g])
        for t in range(3):
            total = total + nn(grads[t][:T1], heads_of(w, g, t))
    (unit,), scale = norm_parts([x[...].astype(F32)])
    into = (own + norm_back([unit], scale, [rounded(total) * gain[...]])[0]).astype(BF)
    units, scale = norm_parts([fine[s * 72 : (s + 1) * 72].astype(F32) for s in range(4)])
    cots = []
    for s in range(4):
        span = slice(s * C0, (s + 1) * C0)
        cots.append(rounded(nt(into, mw[span])) * mgain[:, span])
    backs = jnp.concatenate(norm_back(units, scale, cots), axis=0)
    out[...] = nn(to_window[...], sens[...].astype(F32) + backs).astype(BF)


def window_pack(own, far, at, ch, t):
    span, lanes = slice(at, at + 72), slice(ch, ch + GROUP)
    return jnp.concatenate([own[t, span, lanes].astype(F32), far[t, span, lanes].astype(F32)], axis=0)


def fine_weights(grad, own, far, w, mixed, out):
    mixed[...] = nn(grad[...], w[0]).astype(BF)
    for n, at in enumerate(range(0, T0, 72)):
        for g, ch in enumerate(range(0, C0, GROUP)):
            q, k = [window_pack(own, far, at, ch, t) for t in range(2)]
            out[2 * n + g] = weights_of(q, k).astype(BF)


def fine_back(
    grad, left, right, mixed, weights, own, far, x, to_window, to_nat, gain, w, out
):
    go = grad[...]
    mixed_own = mixed[...].astype(F32)
    mixed_far = jnp.concatenate([rounded(nn(v[...], w[3])) for v in (left, right)], axis=0)
    rows = [[], [], []]
    for n, at in enumerate(range(0, T0, 72)):
        parts = [[], [], []]
        for g, ch in enumerate(range(0, C0, GROUP)):
            span, lanes = slice(at, at + 72), slice(ch, ch + GROUP)
            pack = [window_pack(own, far, at, ch, t) for t in range(3)]
            both = jnp.concatenate([mixed_own[span, lanes], mixed_far[span, lanes]], axis=0)
            grads = mix_back(pack[0], pack[1], pack[2], both, weights[2 * n + g])
            for t in range(3):
                parts[t].append(grads[t][:72])
        for t in range(3):
            rows[t].append(jnp.concatenate(parts[t], axis=1))
    total = sum(nt(jnp.concatenate(rows[t], axis=0), w[t]) for t in range(3))
    (unit,), scale = norm_parts([nn(to_window[...], x[...])])
    back = go.astype(F32) + norm_back([unit], scale, [rounded(total) * gain[...]])[0]
    out[...] = nn(to_nat[...], back).astype(BF)


def local(
    latent_field,
    sensitivity,
    first_gain,
    first_proj,
    merge_gain,
    merge_weight,
    middle_gain,
    middle_proj,
    reduce_gain,
    reduce_weight,
    coarse_gain,
    coarse_proj,
    lift_gain,
    lift_weight,
    widen_gain,
    widen_weight,
):
    lat, lon = lax.axis_index("lat"), lax.axis_index("lon")
    places = [jnp.asarray(table(rule))[lat % 2, lon] for rule in (fellow, member_of)]
    where = jnp.concatenate(places)

    def row(gain):
        return Far(gain.reshape(1, -1))

    def flat(field):
        return field.transpose(0, 2, 1, 3).reshape(T0, C0)

    def unflat(tokens):
        return tokens.reshape(12, 12, 2, C0).transpose(0, 2, 1, 3)

    mid_w = lax.all_gather(middle_proj.transpose(0, 2, 1), "lon", axis=0)
    x = flat(latent_field)
    from_left = send(x[144:], RIGHT)
    from_right = send(x[:144], LEFT)
    reduce_other = send(reduce_weight, NEAR)
    size = C2 // 4

    def quarter(shard, axis):
        return lax.dynamic_slice_in_dim(shard, lat // 2 * size, size, axis)

    lift_part = quarter(lift_weight, 0)
    bundle = send(
        jnp.concatenate([quarter(coarse_proj, 1), lift_part[None, :, :128], lift_part[None, :, 128:]]),
        NEAR,
    )

    def early(start, *operands):
        arrays = after(start, *(v.array for v in operands))[1:]
        return fetch_early(*(v.with_array(array) for v, array in zip(operands, arrays)))

    def order(matrix):
        return Far(jnp.asarray(matrix, BF))

    x, reduce_other, where = after(x, reduce_other, where)
    where = Scalars(where)
    reduce_w = (Far(reduce_weight), Far(reduce_other))
    fine, mid_in, own, far = call(
        fine_forward,
        [((T0, C0), False), ((T1, C1), False), ((3, T0, C0), True), ((3, T0, C0), True)],
        (x, from_left, from_right, order(TO_WINDOW), order(HALF_WINDOW), order(WINDOW_TO_MERGE),
         row(first_gain), Far(first_proj, 4), row(merge_gain), Far(merge_weight, 4)),
    )
    sens, sens_grad = call(
        sens_back,
        [((T0, C0), False), ((T1, C1), False)],
        (flat(sensitivity), order(TO_MERGE), Far(widen_weight)),
    )
    mid_in, bundle = after(mid_in, bundle)
    mid_far = send(mid_in, HALF)
    reduce_later, _ = after(reduce_weight, mid_in)
    (reduce_turned,) = call(turn, [((128, 4 * C1), False)], (Far(reduce_later),))
    others = lax.all_gather(
        bundle, "lat", axis_index_groups=[[p, p + 2, p + 4, p + 6] for p in range(2)], axis=0
    )
    coarse_w = (Far(coarse_proj, 4), Quarters(others, 0, 4))
    lift_w = (Far(lift_weight), Quarters(others, 4, 2))
    mid_far, sens, sens_grad = after(mid_far, sens, sens_grad)
    mid, mid_packed, reduced = call(
        middle_forward,
        [((T1, C1), False), ((3, 2 * T1, C1), True), ((PAD, 4 * C1), False)],
        (mid_in, mid_far, row(middle_gain), Far(mid_w, 4), row(reduce_gain)),
        scratch=[pltpu.VMEM((T1, C1), F32)],
    )
    later, _ = after(reduce_turned, mid)
    reduce_all = lax.all_gather(later, "lon", axis=0)
    rows = 8 * PAD
    near = early(reduced, *reduce_w)
    tokens, near = to_ring(reduced, *near)
    (columns_in,) = call(coarse_reduce, [((rows, 256), False)], (*tokens, *near))


    def halves(width):
        return [((4 * PAD, width), False), ((4 * PAD, width), False)]

    tokens, near = gather8(columns_in, *early(columns_in, *coarse_w))
    even, odd, coarse_packed, coarse_in, coarse_soft = call(
        coarse_forward,
        halves(C2)
        + [((3, rows, 256), False), ((PAD, C2), False), ((rows, 4 * rows), True)],
        (where, *tokens, row(coarse_gain), near[0], JoinedHere(near[1])),
        scratch=[pltpu.VMEM((16, rows, 128), F32)],
        vmem=16,
    )
    packed, _ = after(mid_packed, even)
    (mid_soft,) = call(
        middle_weights, [((4, 2 * T1, 8 * T1), True)], (Far(packed),), vmem=16, beside=4
    )
    coarse_in, mid_soft = after(coarse_in, mid_soft)
    coarse_out, lift_in = call(
        coarse_finish,
        [((PAD, C2), False), ((PAD, C2), False)],
        (*scatter8(even, odd), coarse_in, row(lift_gain)),
    )
    tokens, near = gather8(lift_in, *early(lift_in, *lift_w))
    even, odd = call(lift_forward, halves(512), (*tokens, near[0], JoinedHere(near[1])))
    normed, joined_grad, even, odd = call(
        turn_point,
        [((T1, C1), False), ((T1, C1), False)] + halves(512),
        (where, *exchange8(even, odd, BACK), mid, Far(sens_grad), row(widen_gain)),
        scratch=[pltpu.VMEM((4, T2, C1), F32), pltpu.VMEM((T1, C1), F32)],
    )
    (predicted,) = call(
        widen,
        [((T0, C0), False)],
        (normed, Far(fine), Far(widen_weight), order(TO_MERGE.T)),
        vmem=16,
        beside=4,
    )
    predicted = unflat(predicted)
    near = early(even, *lift_w)
    even, odd = call(
        lift_back, halves(C2), (*exchange8(even, odd, OUT), near[0], JoinedHere(near[1]))
    )
    coarse_out, predicted = after(coarse_out, predicted)
    (coarse_grad,) = call(
        coarse_out_back, [((PAD, C2), False)], (*scatter8(even, odd), coarse_out, row(lift_gain))
    )
    tokens, near = gather8(coarse_grad, *early(coarse_grad, *coarse_w))
    even, odd = call(
        coarse_back,
        halves(C2),
        (*tokens, Far(coarse_packed), Far(coarse_soft), near[0], JoinedHere(near[1])),
        vmem=16,
    )
    (reduce_near,) = early(even, Far(reduce_all))
    (mid_grad,) = call(
        coarse_in_back,
        [((T1, C1), False)],
        (*scatter_back(even, odd), send(jnp.concatenate([coarse_in, coarse_grad]), BACK[0]),
         row(coarse_gain), reduce_near, mid, row(reduce_gain), joined_grad),
        scratch=[pltpu.VMEM((T1, C1), F32), pltpu.VMEM((T1, C1), F32)],
        vmem=16,
    )
    mid_w, merge_weight, _ = after(mid_w, merge_weight, mid_grad)
    mid_near, merge_near = fetch_early(Far(mid_w), Far(merge_weight))
    (fine_grad,) = call(
        middle_back,
        [((T0, C0), False)],
        (mid_grad, send(mid_grad, HALF), mid_in, Far(mid_packed), Far(mid_soft, 4), row(middle_gain),
         mid_near, Far(fine), Far(sens), row(merge_gain), merge_near, order(WINDOW_TO_MERGE.T)),
    )
    grad_left = send(fine_grad[144:], RIGHT)
    grad_right = send(fine_grad[:144], LEFT)
    own, far, _ = after(own, far, fine_grad)
    mixed, fine_soft = call(
        fine_weights,
        [((T0, C0), False), ((8, 2 * T1, 8 * T1), False)],
        (fine_grad, Far(own), Far(far), Far(first_proj[3:])),
        beside=6,
    )
    (result,) = call(
        fine_back,
        [((T0, C0), False)],
        (fine_grad, grad_left, grad_right, mixed, fine_soft, Far(own), Far(far), Far(x),
         order(TO_WINDOW), order(TO_WINDOW.T), row(first_gain), Far(first_proj, 4)),
    )
    return predicted, unflat(result)


def solution(mesh):
    field = P("lon", None, "lat", None)
    placed = (
        field, field, P(), P(), P(), P(), P(), P(None, None, "lon"), P(), P(None, "lon"), P(),
        P(None, None, "lon"), P(), P(None, "lon"), P(), P(),
    )
    return jax.shard_map(
        local, mesh=mesh, in_specs=placed, out_specs=(field, field), check_vma=False
    )
```

```python
import jax
import jax.numpy as jnp
import numpy as np
from jax import lax
from jax.experimental import pallas as pl
from jax.experimental.pallas import tpu as pltpu
from jax.sharding import PartitionSpec as P

BF = jnp.bfloat16
F32 = jnp.float32
EPSILON = 1e-05
HD = 64
GROUP = 4 * HD
LAT, LON = 8, 16
AXES = ("lat", "lon")
T0, T1, T2 = 288, 72, 18
PAD = 24
C0, C1, C2 = 512, 1024, 2048
MIB = 1024 * 1024


def orders():
    window, merge = {}, {}
    for c in range(12):
        for lev in range(2):
            for r in range(12):
                nat = (c * 12 + r) * 2 + lev
                cw, ci, b = c // 6, c % 6 // 2, c % 2
                rw, rj, a = r // 6, r % 6 // 2, r % 2
                s = 2 * a + b
                window[nat] = (cw * 2 + rw) * 72 + s * 18 + (ci * 2 + lev) * 3 + rj
                mc, mr = c // 2, r // 2
                s1 = 2 * (mr % 2) + mc % 2
                merge[nat] = s * 72 + s1 * 18 + (mc // 2 * 2 + lev) * 3 + mr // 2
    to_window = np.zeros((T0, T0), np.float32)
    to_merge = np.zeros((T0, T0), np.float32)
    for nat in range(T0):
        to_window[window[nat], nat] = 1
        to_merge[merge[nat], nat] = 1
    half = np.zeros((144, 144), np.float32)
    for nat in range(144):
        half[window[nat], nat] = 1
    return to_window, half, to_merge


TO_WINDOW, HALF_WINDOW, TO_MERGE = orders()
WINDOW_TO_MERGE = TO_MERGE @ TO_WINDOW.T


ALONG = (0, 1, 3, 2)


def number(lat, lon):
    return lat % LAT * LON + lon % LON


def pairs_of(rule):
    return [(number(a, i), number(*rule(a, i))) for a in range(LAT) for i in range(LON)]


def member_of(lat, lon, k):
    shifted = (lon - 2) % LON
    which = (2 * (lat % 2) + shifted % 4 // 2) ^ k
    return (
        lat // 2 * 2 + which // 2,
        4 * ((shifted // 4 + ALONG[which]) % 4) + 2 * (1 - which % 2) + lon % 2,
    )


def fellow(lat, lon, k):
    which = 2 * (lat % 2) + 1 - lon // 2 % 2
    window = (lon // 4 - ALONG[which]) % 4
    which ^= k
    return (
        lat // 2 * 2 + which // 2,
        4 * ((window + ALONG[which]) % 4) + 2 * (1 - which % 2) + lon % 2,
    )


def table(rule):
    return np.array(
        [[[rule(a, i, k)[1] for k in range(4)] for i in range(LON)] for a in range(2)], np.int32
    )


OUT = [pairs_of(lambda a, i, k=k: member_of(a, i, k)) for k in range(4)]
BACK = [[(target, source) for source, target in pairs] for pairs in OUT]
RING = [pairs_of(lambda a, i, k=k: fellow(a, i, k)) for k in range(4)]
CORE = pairs_of(lambda a, i: (a, i ^ 1))
NEAR = pairs_of(lambda a, i: (a ^ 1, i ^ 2))
RIGHT = pairs_of(lambda a, i: (a, i + 1))
LEFT = pairs_of(lambda a, i: (a, i - 1))
HALF = pairs_of(lambda a, i: (a, i + 1 if i % 2 else i - 1))


def send(value, pairs):
    return lax.ppermute(value, AXES, pairs)


def after(value, *others):
    return lax.optimization_barrier((value, *others))


def across(parts, meanwhile):
    chips, *meanwhile = after(jnp.concatenate(parts), *meanwhile)
    return (chips, send(chips, CORE)), meanwhile


def to_ring(block, *meanwhile):
    return across([send(block, OUT[k]) for k in range(4)], meanwhile)


def gather8(block, *meanwhile):
    return across([block] + [send(block, RING[k]) for k in (1, 2, 3)], meanwhile)


def chip_sums(even, odd):
    both = (even.astype(F32) + send(odd, CORE).astype(F32)).astype(BF)
    return [both[k * PAD : (k + 1) * PAD] for k in range(4)]


def scatter8(even, odd):
    parts = chip_sums(even, odd)
    return [parts[0]] + [send(parts[k], RING[k]) for k in (1, 2, 3)]


def scatter_back(even, odd):
    return [send(part, BACK[k]) for k, part in enumerate(chip_sums(even, odd))]


def exchange8(even, odd, ways):
    other = send(odd, CORE)
    return [
        send(jnp.concatenate([even[k * PAD : (k + 1) * PAD], other[k * PAD : (k + 1) * PAD]]), ways[k])
        for k in range(4)
    ]


def nn(a, b):
    return lax.dot_general(
        a.astype(BF), b.astype(BF), (((1,), (0,)), ((), ())), preferred_element_type=F32
    )


def nt(a, b):
    return lax.dot_general(
        a.astype(BF), b.astype(BF), (((1,), (1,)), ((), ())), preferred_element_type=F32
    )


def tn(a, b):
    return lax.dot_general(
        a.astype(BF), b.astype(BF), (((0,), (0,)), ((), ())), preferred_element_type=F32
    )


def rounded(value):
    return value.astype(BF).astype(F32)


def norm_parts(pieces):
    width = sum(v.shape[1] for v in pieces)
    mean = sum(jnp.sum(v, axis=1, keepdims=True) for v in pieces) / width
    centred = [v - mean for v in pieces]
    spread = sum(jnp.sum(v * v, axis=1, keepdims=True) for v in centred) / width
    scale = lax.rsqrt(spread + EPSILON)
    return [v * scale for v in centred], scale


def norm_back(unit, scale, cot):
    width = sum(v.shape[1] for v in unit)
    first = sum(jnp.sum(v, axis=1, keepdims=True) for v in cot) / width
    second = sum(jnp.sum(v * u, axis=1, keepdims=True) for v, u in zip(cot, unit)) / width
    return [scale * (v - first - u * second) for v, u in zip(cot, unit)]


def head_masks():
    lane = lax.broadcasted_iota(jnp.int32, (1, GROUP), 1) // HD
    return [(lane == h).astype(F32) for h in range(4)]


def by_head(value):
    return jnp.concatenate([value * m for m in head_masks()], axis=0)


def own_heads(value, rows):
    return sum(value[h * rows : (h + 1) * rows] * m for h, m in enumerate(head_masks()))


def weights_of(q, k, dead=None):
    scores = nt(k, by_head(q)) * HD ** (-0.5)
    if dead is not None:
        scores = jnp.where(dead, -1e30, scores)
    raised = jnp.exp(scores - jnp.max(scores, axis=0, keepdims=True))
    return raised / jnp.sum(raised, axis=0, keepdims=True)


def mix(weights, v, rows):
    return rounded(own_heads(tn(weights, v), rows))


def mix_back(q, k, v, grad, weights):
    grads = by_head(grad)
    from_weights = nt(v, grads)
    soft = weights.astype(F32)
    inner = jnp.sum(soft * from_weights, axis=0, keepdims=True)
    from_scores = soft * (from_weights - inner) * HD ** (-0.5)
    return (
        rounded(own_heads(tn(from_scores, k), q.shape[0])),
        rounded(nn(from_scores, by_head(q))),
        rounded(nn(weights, grads)),
    )


class Scalars:
    def __init__(self, array):
        self.array = array


class Far:
    def __init__(self, array, parts=1):
        self.array, self.parts = array, parts

    def with_array(self, array):
        return Far(array, self.parts)


class Quarters:
    def __init__(self, array, first, count):
        self.array, self.first, self.count = array, first, count

    def with_array(self, array):
        return Quarters(array, self.first, self.count)


class JoinedHere:
    def __init__(self, array):
        self.array = array


class Rows:
    def __init__(self, ref):
        self.ref = ref

    def __getitem__(self, t):
        value = self.ref[t]
        return value.reshape(-1, value.shape[-1])


class Fetched:
    def __init__(self, source, held, sems, parts):
        self.held, self.size = held, source.shape[0] // parts
        self.copies = [
            pltpu.make_async_copy(
                source.at[pl.ds(n * self.size, self.size)],
                held.at[pl.ds(n * self.size, self.size)],
                sems.at[n],
            )
            for n in range(parts)
        ]
        for copy in self.copies:
            copy.start()
        self.waiting = set(range(parts))

    def __getitem__(self, at):
        lead = at[0] if isinstance(at, tuple) else at
        if isinstance(lead, int):
            wanted = {lead // self.size}
        elif isinstance(lead, slice):
            first, last, _ = lead.indices(self.held.shape[0])
            wanted = set(range(first // self.size, (last - 1) // self.size + 1))
        else:
            wanted = set(self.waiting)
        for n in sorted(wanted & self.waiting):
            self.copies[n].wait()
        self.waiting -= wanted
        return self.held[at]


class Kept:
    def __init__(self, target, held, sem):
        self.held, self.copy, self.open = held, pltpu.make_async_copy(held, target, sem), True

    def __setitem__(self, at, value):
        self.held[at] = value

    def flush(self):
        self.open = False
        self.copy.start()


def cost_of(microseconds):
    return pl.CostEstimate(
        flops=1 + microseconds * 10**9, bytes_accessed=1 + microseconds * 10**6 * 3, transcendentals=0
    )


def call(body, outs, args, scratch=(), vmem=24, beside=0):
    specs, arrays, extra = [], [], []
    for arg in args:
        if isinstance(arg, Scalars):
            specs.append(pl.BlockSpec(memory_space=pltpu.SMEM))
            arrays.append(arg.array)
        elif isinstance(arg, Far):
            specs.append(pl.BlockSpec(memory_space=pltpu.HBM))
            arrays.append(pltpu.with_memory_space_constraint(arg.array, pltpu.HBM))
            extra.append(pltpu.VMEM(arg.array.shape, arg.array.dtype))
            extra.append(pltpu.SemaphoreType.DMA((arg.parts,)))
        else:
            specs.append(pl.BlockSpec(memory_space=pltpu.VMEM))
            arrays.append(arg.array if isinstance(arg, JoinedHere) else arg)
    for shape, own in outs:
        if own:
            extra.append(pltpu.VMEM(shape, BF))
            extra.append(pltpu.SemaphoreType.DMA)

    def kernel(*refs):
        ins, rest = list(refs[: len(specs)]), refs[len(specs) :]
        targets, rest = rest[: len(outs)], rest[len(outs) :]
        buffers, rest = rest[: len(scratch)], list(rest[len(scratch) :])
        given = []
        for arg in args:
            ref = ins.pop(0)
            if isinstance(arg, Far):
                given.append(Fetched(ref, rest.pop(0), rest.pop(0), arg.parts))
            else:
                given.append(Rows(ref) if isinstance(arg, JoinedHere) else ref)
        kept = []
        for (_, own), ref in zip(outs, targets):
            kept.append(Kept(ref, rest.pop(0), rest.pop(0)) if own else ref)
        body(*given, *kept, *buffers)
        for held in kept:
            if isinstance(held, Kept):
                if held.open:
                    held.flush()
                held.copy.wait()
        for held in given:
            if isinstance(held, Fetched):
                for n in sorted(held.waiting):
                    held.copies[n].wait()

    return pl.pallas_call(
        kernel,
        out_shape=[
            pltpu.HBM(shape, BF) if own else jax.ShapeDtypeStruct(shape, BF) for shape, own in outs
        ],
        in_specs=specs,
        out_specs=[
            pl.BlockSpec(memory_space=pltpu.HBM if own else pltpu.VMEM) for _, own in outs
        ],
        scratch_shapes=list(scratch) + extra,
        compiler_params=pltpu.CompilerParams(vmem_limit_bytes=vmem * MIB),
        cost_estimate=cost_of(beside),
    )(*arrays)


def fetch_early(*arrays):
    def kernel(*refs):
        count = len(arrays)
        copies = []
        for n, arg in enumerate(arrays):
            source, target, sems = refs[n], refs[count + n], refs[2 * count + n]
            if isinstance(arg, Quarters):
                parts = [(source.at[:, arg.first + t], target.at[t]) for t in range(arg.count)]
            else:
                size = source.shape[0] // 4
                spans = [pl.ds(t * size, size) for t in range(4)]
                parts = [(source.at[span], target.at[span]) for span in spans]
            for t, (part, place) in enumerate(parts):
                copies.append(pltpu.make_async_copy(part, place, sems.at[t]))
                copies[-1].start()
        for copy in copies:
            copy.wait()

    shapes = [
        (v.count, 4, *v.array.shape[2:]) if isinstance(v, Quarters) else v.array.shape for v in arrays
    ]
    outs = pl.pallas_call(
        kernel,
        out_shape=[pltpu.VMEM(shape, BF) for shape in shapes],
        in_specs=[pl.BlockSpec(memory_space=pltpu.HBM)] * len(arrays),
        out_specs=[pl.BlockSpec(memory_space=pltpu.VMEM)] * len(arrays),
        scratch_shapes=[pltpu.SemaphoreType.DMA((4,))] * len(arrays),
        compiler_params=pltpu.CompilerParams(vmem_limit_bytes=4 * MIB),
        cost_estimate=cost_of(4),
    )(*[pltpu.with_memory_space_constraint(v.array, pltpu.HBM) for v in arrays])
    return list(outs)


def turn(w, out):
    row = lax.broadcasted_iota(jnp.int32, (128, 128), 0)
    column = lax.broadcasted_iota(jnp.int32, (128, 128), 1)
    pick = (row == column).astype(BF)
    for j in range(8):
        out[:, j * 512 : (j + 1) * 512] = nt(pick, w[j * 512 : (j + 1) * 512]).astype(BF)


def fine_forward(x, left, right, to_window, half, to_merge, gain, w, mgain, mw, fine, mid, own, far):
    xo = nn(to_window[...], x[...])
    xh = jnp.concatenate([nn(half[...], left[...]), nn(half[...], right[...])], axis=0)
    packs = []
    for value, kept in ((xo, own), (xh, far)):
        (unit,), _ = norm_parts([value])
        normed = (unit * gain[...]).astype(BF)
        pack = [rounded(nn(normed, w[t])) for t in range(3)]
        for t in range(3):
            kept[t] = pack[t].astype(BF)
        kept.flush()
        packs.append(pack)
    rows = []
    for at in range(0, T0, 72):
        parts = []
        for ch in range(0, C0, GROUP):
            q = packs[0][0][at : at + 72, ch : ch + GROUP]
            k, v = [
                jnp.concatenate([pk[t][at : at + 72, ch : ch + GROUP] for pk in packs], axis=0)
                for t in (1, 2)
            ]
            parts.append(mix(weights_of(q, k), v, 72))
        rows.append(jnp.concatenate(parts, axis=1))
    mixed = jnp.concatenate(rows, axis=0)
    out = rounded(xo + nt(mixed, w[3]))
    merged = nn(to_merge[...], out)
    fine[...] = merged.astype(BF)
    units, _ = norm_parts([merged[s * 72 : (s + 1) * 72] for s in range(4)])
    total = 0.0
    for s in range(4):
        span = slice(s * C0, (s + 1) * C0)
        total = total + nn(units[s] * mgain[:, span], mw[span])
    mid[...] = total.astype(BF)


def heads_of(w, g, t):
    return jnp.concatenate([w[4 * g + h, t] for h in range(4)], axis=0)


def middle_forward(x, partner, gain, w, rgain, out, packed, reduced, buf, rest):
    own = x[...].astype(F32)
    both = jnp.concatenate([own, partner[...].astype(F32)], axis=0)
    (unit,), _ = norm_parts([both])
    normed = (unit * gain[...]).astype(BF)
    total = own
    for g in range(4):
        span = slice(g * GROUP, (g + 1) * GROUP)
        pack = [rounded(nt(normed, heads_of(w, g, t))) for t in range(3)]
        for t in range(3):
            packed[t, :, span] = pack[t].astype(BF)
        total = total + nn(mix(weights_of(pack[0][:T1], pack[1]), pack[2], T1), heads_of(w, g, 3))
    out[...] = total.astype(BF)
    buf[...] = rounded(total)
    units, _ = norm_parts([buf[s * T2 : (s + 1) * T2] for s in range(4)])
    for s in range(4):
        span = slice(s * C1, (s + 1) * C1)
        value = units[s] * rgain[:, span]
        reduced[:, span] = value[:16].astype(BF)
        for t in range(2):
            for h in range(2):
                at = 8 * t + 2 * s + h
                rest[at : at + 1] = value[16 + t : 17 + t, h * 512 : (h + 1) * 512]
    reduced[:, 4 * C1 :] = rest[...].astype(BF)


def below(parts):
    return jnp.concatenate([part[...] for part in parts], axis=0)


def halves_out(value, even, odd):
    even[...] = value[: 4 * PAD].astype(BF)
    odd[...] = value[4 * PAD :].astype(BF)


def coarse_reduce(chips, mates, own, other, out, buf):
    tokens = below((chips, mates))
    w = jnp.concatenate([own[...], other[...]], axis=1)
    first = nn(tokens[:, : 4 * C1], w)
    rest = tokens[:, 4 * C1 :].astype(F32)
    part = lax.broadcasted_iota(jnp.int32, (128, 1), 0) % 8
    last = 0.0
    for n in range(8):
        last = last + nn(jnp.where(part == n, rest, 0.0), w[n * 512 : (n + 1) * 512])
    last = jnp.sum(last.reshape(16, 8, 256), axis=1)
    buf[...] = jnp.zeros_like(buf)
    for k in range(8):
        buf[k * PAD : k * PAD + 16] = first[k * 16 : (k + 1) * 16]
        buf[k * PAD + 16 : k * PAD + T2] = last[2 * k : 2 * k + 2]
    out[...] = buf[...].astype(BF)


def dead_keys():
    return lax.broadcasted_iota(jnp.int32, (8 * PAD, 1), 0) % PAD >= T2


def coarse_heads(own, others, t):
    return jnp.concatenate([own[t], others[t]], axis=1)


def coarse_forward(where, chips, mates, gain, own, others, even, odd, packed, kept, soft, buf):
    for e, source in enumerate((chips, mates)):
        for d in range(4):
            columns = source[d * 8 * PAD : (d + 1) * 8 * PAD].astype(F32)
            for at in range(8):
                rows = columns[at * PAD : (at + 1) * PAD]
                to = ((at // 4 ^ e) * 4 + (at % 4 ^ d)) * PAD
                for r in range(2):
                    buf[where[d] ^ (2 * r + e), to : to + PAD] = rows[:, r * 128 : (r + 1) * 128]
    pieces = [buf[n] for n in range(16)]
    units, _ = norm_parts(pieces)
    normed = []
    for n in range(16):
        lanes = slice(n * 128, (n + 1) * 128)
        kept[:, lanes] = pieces[n][:PAD].astype(BF)
        normed.append((units[n] * gain[:, lanes]).astype(BF))
    normed = jnp.concatenate(normed, axis=1)
    pack = [rounded(nn(normed, coarse_heads(own, others, t))) for t in range(3)]
    for t in range(3):
        packed[t] = pack[t].astype(BF)
    weights = weights_of(pack[0], pack[1], dead_keys())
    soft[...] = weights.astype(BF)
    mixed = mix(weights, pack[2], 8 * PAD)
    halves_out(nt(mixed, coarse_heads(own, others, 3)), even, odd)


def total_of(parts):
    return sum(p[...].astype(F32) for p in parts)


def coarse_finish(a, b, c, d, x, gain, out, normed):
    value = rounded(x[...].astype(F32) + total_of((a, b, c, d)))
    out[...] = value.astype(BF)
    (unit,), _ = norm_parts([value])
    normed[...] = (unit * gain[...]).astype(BF)


def shards_of(own, first, second):
    low, high = [second[0, :, at : at + 256].reshape(-1, 128) for at in (0, 256)]
    other = jnp.concatenate([first[...], jnp.concatenate([low, high], axis=1)], axis=0)
    return jnp.concatenate([own[...], other], axis=1)


def lift_forward(chips, mates, own, first, second, even, odd):
    tokens = below((chips, mates))
    columns = nn(tokens, shards_of(own, first, second))
    halves_out(columns, even, odd)


def sens_back(sens, to_merge, ww, merged, grad):
    value = nn(to_merge[...], sens[...])
    merged[...] = value.astype(BF)
    total = 0.0
    for s in range(4):
        total = total + nt(value[s * 72 : (s + 1) * 72], ww[:, s * C0 : (s + 1) * C0])
    grad[...] = total.astype(BF)


def member_lanes(where, k, e, r):
    return pl.multiple_of((where[4 + k] % 4 ^ (2 * r + e)) * 256, 256)


def turn_point(
    where, a, b, c, d, mid, grad, gain, out, joined_grad, even, odd, wide, flat
):
    for k, source in enumerate((a, b, c, d)):
        block = source[...].astype(F32)
        for e in range(2):
            rows = block[e * PAD : e * PAD + T2]
            for r in range(2):
                wide[where[4 + k] // 4, :, pl.ds(member_lanes(where, k, e, r), 256)] = rows[
                    :, r * 256 : (r + 1) * 256
                ]
    for s in range(4):
        flat[s * T2 : (s + 1) * T2] = wide[s]
    joined = rounded(mid[...].astype(F32) + flat[...])
    (unit,), scale = norm_parts([joined])
    out[...] = (unit * gain[...]).astype(BF)
    (back,) = norm_back([unit], scale, [grad[...].astype(F32) * gain[...]])
    joined_grad[...] = back.astype(BF)
    flat[...] = rounded(back)
    for s in range(4):
        wide[s] = flat[s * T2 : (s + 1) * T2]
    for e, target in enumerate((even, odd)):
        target[...] = jnp.zeros_like(target)
        for k in range(4):
            for r in range(2):
                target[k * PAD : k * PAD + T2, r * 256 : (r + 1) * 256] = wide[
                    where[4 + k] // 4, :, pl.ds(member_lanes(where, k, e, r), 256)
                ].astype(BF)


def widen(normed, fine, ww, to_nat, out):
    rows = [
        fine[s * 72 : (s + 1) * 72].astype(F32) + nn(normed[...], ww[:, s * C0 : (s + 1) * C0])
        for s in range(4)
    ]
    out[...] = nn(to_nat[...], jnp.concatenate(rows, axis=0)).astype(BF)


def lift_back(a, b, c, d, own, first, second, even, odd):
    blocks = [v[...].astype(F32) for v in (a, b, c, d)]
    tokens = jnp.concatenate([v[:PAD] for v in blocks] + [v[PAD:] for v in blocks], axis=0)
    halves_out(nt(tokens, shards_of(own, first, second)), even, odd)


def coarse_out_back(a, b, c, d, value, gain, out):
    (unit,), scale = norm_parts([value[...].astype(F32)])
    cot = rounded(total_of((a, b, c, d))) * gain[...]
    out[...] = norm_back([unit], scale, [cot])[0].astype(BF)


def coarse_back(chips, mates, packed, weights, own, others, even, odd):
    grad = rounded(nn(below((chips, mates)), coarse_heads(own, others, 3)))
    pack = [packed[t].astype(F32) for t in range(3)]
    grads = mix_back(pack[0], pack[1], pack[2], grad, weights[...])
    halves_out(sum(nt(grads[t], coarse_heads(own, others, t)) for t in range(3)), even, odd)


def coarse_in_back(a, b, c, d, pair, gain, w, mid, mid_gain, mid_grad, out, buf, back):
    (unit,), scale = norm_parts([pair[:PAD].astype(F32)])
    cot = rounded(total_of((a, b, c, d))) * gain[...]
    cot = (pair[PAD:].astype(F32) + norm_back([unit], scale, [cot])[0]).astype(BF)
    total = 0.0
    for n in range(8):
        total = total + nn(cot[:, n * 256 : (n + 1) * 256], w[2 * n : 2 * n + 2].reshape(256, -1))
    buf[...] = mid[...].astype(F32)
    units, scale = norm_parts([buf[s * T2 : (s + 1) * T2] for s in range(4)])
    cot = rounded(total[:T2]) * mid_gain[...]
    backs = norm_back(units, scale, [cot[:, s * C1 : (s + 1) * C1] for s in range(4)])
    for s in range(4):
        back[s * T2 : (s + 1) * T2] = backs[s]
    out[...] = (mid_grad[...].astype(F32) + back[...]).astype(BF)


def middle_weights(packed, out):
    for g in range(4):
        span = slice(g * GROUP, (g + 1) * GROUP)
        q, k = [packed[t, :, span].astype(F32) for t in range(2)]
        out[g] = weights_of(q, k).astype(BF)


def middle_back(grad, partner, x, packed, weights, gain, w, fine, sens, mgain, mw, to_window, out):
    own = grad[...].astype(F32)
    both = jnp.concatenate([own, partner[...].astype(F32)], axis=0)
    total = 0.0
    for g in range(4):
        span = slice(g * GROUP, (g + 1) * GROUP)
        mixed = rounded(nt(both, heads_of(w, g, 3)))
        pack = [packed[t, :, span].astype(F32) for t in range(3)]
        grads = mix_back(pack[0], pack[1], pack[2], mixed, weights[g])
        for t in range(3):
            total = total + nn(grads[t][:T1], heads_of(w, g, t))
    (unit,), scale = norm_parts([x[...].astype(F32)])
    into = (own + norm_back([unit], scale, [rounded(total) * gain[...]])[0]).astype(BF)
    units, scale = norm_parts([fine[s * 72 : (s + 1) * 72].astype(F32) for s in range(4)])
    cots = []
    for s in range(4):
        span = slice(s * C0, (s + 1) * C0)
        cots.append(rounded(nt(into, mw[span])) * mgain[:, span])
    backs = jnp.concatenate(norm_back(units, scale, cots), axis=0)
    out[...] = nn(to_window[...], sens[...].astype(F32) + backs).astype(BF)


def window_pack(own, far, at, ch, t):
    span, lanes = slice(at, at + 72), slice(ch, ch + GROUP)
    return jnp.concatenate([own[t, span, lanes].astype(F32), far[t, span, lanes].astype(F32)], axis=0)


def fine_weights(grad, own, far, w, mixed, out):
    mixed[...] = nn(grad[...], w[0]).astype(BF)
    for n, at in enumerate(range(0, T0, 72)):
        for g, ch in enumerate(range(0, C0, GROUP)):
            q, k = [window_pack(own, far, at, ch, t) for t in range(2)]
            out[2 * n + g] = weights_of(q, k).astype(BF)


def fine_back(
    grad, left, right, mixed, weights, own, far, x, to_window, to_nat, gain, w, out
):
    go = grad[...]
    mixed_own = mixed[...].astype(F32)
    mixed_far = jnp.concatenate([rounded(nn(v[...], w[3])) for v in (left, right)], axis=0)
    rows = [[], [], []]
    for n, at in enumerate(range(0, T0, 72)):
        parts = [[], [], []]
        for g, ch in enumerate(range(0, C0, GROUP)):
            span, lanes = slice(at, at + 72), slice(ch, ch + GROUP)
            pack = [window_pack(own, far, at, ch, t) for t in range(3)]
            both = jnp.concatenate([mixed_own[span, lanes], mixed_far[span, lanes]], axis=0)
            grads = mix_back(pack[0], pack[1], pack[2], both, weights[2 * n + g])
            for t in range(3):
                parts[t].append(grads[t][:72])
        for t in range(3):
            rows[t].append(jnp.concatenate(parts[t], axis=1))
    total = sum(nt(jnp.concatenate(rows[t], axis=0), w[t]) for t in range(3))
    (unit,), scale = norm_parts([nn(to_window[...], x[...])])
    back = go.astype(F32) + norm_back([unit], scale, [rounded(total) * gain[...]])[0]
    out[...] = nn(to_nat[...], back).astype(BF)


def local(
    latent_field,
    sensitivity,
    first_gain,
    first_proj,
    merge_gain,
    merge_weight,
    middle_gain,
    middle_proj,
    reduce_gain,
    reduce_weight,
    coarse_gain,
    coarse_proj,
    lift_gain,
    lift_weight,
    widen_gain,
    widen_weight,
):
    lat, lon = lax.axis_index("lat"), lax.axis_index("lon")
    places = [jnp.asarray(table(rule))[lat % 2, lon] for rule in (fellow, member_of)]
    where = jnp.concatenate(places)

    def row(gain):
        return Far(gain.reshape(1, -1))

    def flat(field):
        return field.transpose(0, 2, 1, 3).reshape(T0, C0)

    def unflat(tokens):
        return tokens.reshape(12, 12, 2, C0).transpose(0, 2, 1, 3)

    mid_w = lax.all_gather(middle_proj.transpose(0, 2, 1), "lon", axis=0)
    x = flat(latent_field)
    from_left = send(x[144:], RIGHT)
    from_right = send(x[:144], LEFT)
    def quarter(shard, axis):
        size = shard.shape[axis] // 4
        return lax.dynamic_slice_in_dim(shard, lat // 2 * size, size, axis)

    reduce_other = send(reduce_weight, NEAR)
    part = quarter(lift_weight[C2 // 2 :], 0)
    part = jnp.concatenate([part[:, :128], part[:, 128:]])
    bundle = send(jnp.concatenate([quarter(coarse_proj, 1), part[None]]), NEAR)
    lift_other = send(lift_weight[: C2 // 2], NEAR)

    def early(start, *operands):
        arrays = after(start, *(v.array for v in operands))[1:]
        return fetch_early(*(v.with_array(array) for v, array in zip(operands, arrays)))

    def order(matrix):
        return Far(jnp.asarray(matrix, BF))

    x, reduce_other, where = after(x, reduce_other, where)
    where = Scalars(where)
    reduce_w = (Far(reduce_weight), Far(reduce_other))
    fine, mid_in, own, far = call(
        fine_forward,
        [((T0, C0), False), ((T1, C1), False), ((3, T0, C0), True), ((3, T0, C0), True)],
        (x, from_left, from_right, order(TO_WINDOW), order(HALF_WINDOW), order(WINDOW_TO_MERGE),
         row(first_gain), Far(first_proj, 4), row(merge_gain), Far(merge_weight, 4)),
    )
    sens, sens_grad = call(
        sens_back,
        [((T0, C0), False), ((T1, C1), False)],
        (flat(sensitivity), order(TO_MERGE), Far(widen_weight)),
    )
    mid_in, bundle = after(mid_in, bundle)
    mid_far = send(mid_in, HALF)
    reduce_later, _ = after(reduce_weight, mid_in)
    (reduce_turned,) = call(turn, [((128, 4 * C1), False)], (Far(reduce_later),))
    others = lax.all_gather(
        bundle, "lat", axis_index_groups=[[p, p + 2, p + 4, p + 6] for p in range(2)], axis=0
    )
    coarse_w = (Far(coarse_proj, 4), Quarters(others, 0, 4))
    mid_far, lift_other = after(mid_far, lift_other)
    lift_w = (Far(lift_weight), Far(lift_other), Quarters(others, 4, 1))
    mid_far, sens, sens_grad = after(mid_far, sens, sens_grad)
    mid, mid_packed, reduced = call(
        middle_forward,
        [((T1, C1), False), ((3, 2 * T1, C1), True), ((16, 4 * C1 + 512), False)],
        (mid_in, mid_far, row(middle_gain), Far(mid_w, 4), row(reduce_gain)),
        scratch=[pltpu.VMEM((T1, C1), F32), pltpu.VMEM((16, 512), F32)],
    )
    later, _ = after(reduce_turned, mid)
    reduce_all = lax.all_gather(later, "lon", axis=0)
    rows = 8 * PAD
    near = early(reduced, *reduce_w)
    tokens, near = to_ring(reduced, *near)
    (columns_in,) = call(
        coarse_reduce,
        [((rows, 256), False)],
        (*tokens, *near),
        scratch=[pltpu.VMEM((rows, 256), F32)],
        vmem=16,
    )


    def halves(width):
        return [((4 * PAD, width), False), ((4 * PAD, width), False)]

    tokens, near = gather8(columns_in, *early(columns_in, *coarse_w))
    even, odd, coarse_packed, coarse_in, coarse_soft = call(
        coarse_forward,
        halves(C2)
        + [((3, rows, 256), False), ((PAD, C2), False), ((rows, 4 * rows), True)],
        (where, *tokens, row(coarse_gain), near[0], JoinedHere(near[1])),
        scratch=[pltpu.VMEM((16, rows, 128), F32)],
        vmem=16,
    )
    packed, _ = after(mid_packed, even)
    (mid_soft,) = call(
        middle_weights, [((4, 2 * T1, 8 * T1), True)], (Far(packed),), vmem=16, beside=4
    )
    coarse_in, mid_soft = after(coarse_in, mid_soft)
    coarse_out, lift_in = call(
        coarse_finish,
        [((PAD, C2), False), ((PAD, C2), False)],
        (*scatter8(even, odd), coarse_in, row(lift_gain)),
    )
    tokens, near = gather8(lift_in, *early(lift_in, *lift_w))
    even, odd = call(lift_forward, halves(512), (*tokens, *near))
    normed, joined_grad, even, odd = call(
        turn_point,
        [((T1, C1), False), ((T1, C1), False)] + halves(512),
        (where, *exchange8(even, odd, BACK), mid, Far(sens_grad), row(widen_gain)),
        scratch=[pltpu.VMEM((4, T2, C1), F32), pltpu.VMEM((T1, C1), F32)],
    )
    (predicted,) = call(
        widen,
        [((T0, C0), False)],
        (normed, Far(fine), Far(widen_weight), order(TO_MERGE.T)),
        vmem=16,
        beside=4,
    )
    predicted = unflat(predicted)
    near = early(even, *lift_w)
    even, odd = call(lift_back, halves(C2), (*exchange8(even, odd, OUT), *near))
    coarse_out, predicted = after(coarse_out, predicted)
    (coarse_grad,) = call(
        coarse_out_back, [((PAD, C2), False)], (*scatter8(even, odd), coarse_out, row(lift_gain))
    )
    tokens, near = gather8(coarse_grad, *early(coarse_grad, *coarse_w))
    even, odd = call(
        coarse_back,
        halves(C2),
        (*tokens, Far(coarse_packed), Far(coarse_soft), near[0], JoinedHere(near[1])),
        vmem=16,
    )
    (reduce_near,) = early(even, Far(reduce_all))
    (mid_grad,) = call(
        coarse_in_back,
        [((T1, C1), False)],
        (*scatter_back(even, odd), send(jnp.concatenate([coarse_in, coarse_grad]), BACK[0]),
         row(coarse_gain), reduce_near, mid, row(reduce_gain), joined_grad),
        scratch=[pltpu.VMEM((T1, C1), F32), pltpu.VMEM((T1, C1), F32)],
        vmem=16,
    )
    mid_w, merge_weight, _ = after(mid_w, merge_weight, mid_grad)
    mid_near, merge_near = fetch_early(Far(mid_w), Far(merge_weight))
    (fine_grad,) = call(
        middle_back,
        [((T0, C0), False)],
        (mid_grad, send(mid_grad, HALF), mid_in, Far(mid_packed), Far(mid_soft, 4), row(middle_gain),
         mid_near, Far(fine), Far(sens), row(merge_gain), merge_near, order(WINDOW_TO_MERGE.T)),
    )
    grad_left = send(fine_grad[144:], RIGHT)
    grad_right = send(fine_grad[:144], LEFT)
    own, far, _ = after(own, far, fine_grad)
    mixed, fine_soft = call(
        fine_weights,
        [((T0, C0), False), ((8, 2 * T1, 8 * T1), False)],
        (fine_grad, Far(own), Far(far), Far(first_proj[3:])),
        beside=6,
    )
    (result,) = call(
        fine_back,
        [((T0, C0), False)],
        (fine_grad, grad_left, grad_right, mixed, fine_soft, Far(own), Far(far), Far(x),
         order(TO_WINDOW), order(TO_WINDOW.T), row(first_gain), Far(first_proj, 4)),
    )
    return predicted, unflat(result)


def solution(mesh):
    field = P("lon", None, "lat", None)
    placed = (
        field, field, P(), P(), P(), P(), P(), P(None, None, "lon"), P(), P(None, "lon"), P(),
        P(None, None, "lon"), P(), P(None, "lon"), P(), P(),
    )
    return jax.shard_map(
        local, mesh=mesh, in_specs=placed, out_specs=(field, field), check_vma=False
    )
```
